128 devices in a mesh: ctx: 16 (over y, z_lo, core), head: 8 (over z_hi, x).
Axes of the slice: x: 4, y: 4, z: 4 (z_hi: 2, z_lo: 2; z = z_hi * 2 + z_lo), core: 2. Of those that a mesh axis runs over, the one named last changes fastest.
Arguments:
- q_nope: bfloat16 [1024, 8192], P('ctx', 'head'), may hold values from -0.59765625 to 0.59765625
- q_rope: bfloat16 [1024, 4096], P('ctx', 'head'), may hold values from -6 to 6
- w_uk: bfloat16 [64, 128, 512], P('head'), may hold values from -0.5 to 0.5
- w_uv: bfloat16 [64, 512, 128], P('head'), may hold values from -0.25 to 0.25
- w_o: bfloat16 [8192, 7168], P('head'), may hold values from -0.0625 to 0.0625
- latent_cache: bfloat16 [576, 16384], P(None, 'ctx'), may hold values from -36 to 36
- group_start: int32 [1], replicated, may hold values from 4096 to 15360
Outputs:
- attention_out: bfloat16 [1024, 7168], P('ctx', 'head')
The draws below stay inside these ranges and needn't reach their ends.
All inputs are finite; a program needn't handle non-finite values.
Results may differ from the reference program's by a relative error of at most 0.02.
Values may be sent and summed in bfloat16 or wider, within the bound.
No kernel may reach another device: no remote copies, remote signals or barrier semaphores. Data moves between devices by JAX's collectives and lax.ppermute only.
A program may use at most 128 MiB of HBM per device.

```python
import math
import jax
import jax.numpy as jnp
from jax import lax

D = 7168
HEADS = 64
LATENT = 512
ROPE = 64
NOPE = 128
VDIM = 128
GROUP = 1024
CACHE = 16384


def draw_latent_cache(key, part):
    latent_part = jnp.clip(6.0 * jax.random.normal(jax.random.fold_in(key, 821), (LATENT, CACHE), jnp.float32), -36.0, 36.0)
    rope_part = jnp.clip(jax.random.normal(jax.random.fold_in(key, 822), (ROPE, CACHE), jnp.float32), -6.0, 6.0)
    return jnp.concatenate([latent_part, rope_part], axis=0).astype(jnp.bfloat16)


def draw_q_rope(key, part):
    rope_query = jnp.clip(jax.random.normal(jax.random.fold_in(key, 831), (GROUP, HEADS, ROPE), jnp.float32), -6.0, 6.0)
    return rope_query.reshape(GROUP, HEADS * ROPE).astype(jnp.bfloat16)


def shard_levels(own_key, dims, cuts, low, top_value):
    gain, own = 1.0, jax.random.fold_in(own_key, 6)
    for dim, shards_of in cuts:
        draws = jnp.exp(jax.random.uniform(jax.random.fold_in(own, dim), (shards_of,), jnp.float32, low / len(cuts), top_value / len(cuts)))
        gain = gain * jnp.repeat(draws, dims[dim] // shards_of).reshape([-1 if axis == dim else 1 for axis in range(len(dims))])
    return gain


def noise(rng, extent, spread, reach, cuts=(), kind=jnp.bfloat16):
    values = jax.random.normal(rng, extent, jnp.float32) * spread
    if len(cuts) > 0:
        values = shard_levels(rng, extent, cuts, -0.22, 0.18) * values
    return jnp.clip(values, min=-reach, max=reach).astype(kind)


def setup_inputs(seed: int = 0) -> dict:
    arg_keys = jax.random.split(jax.random.key(seed), 8)
    return {
        "q_nope": noise(arg_keys[0], (GROUP, HEADS * NOPE), 0.1, 0.59765625, ((0, 16), (1, 8))),
        "q_rope": draw_q_rope(jax.random.fold_in(arg_keys[7], 71), 0),
        "w_uk": noise(arg_keys[2], (HEADS, NOPE, LATENT), NOPE ** -0.5, 0.5, ((0, 8),)),
        "w_uv": noise(arg_keys[3], (HEADS, LATENT, VDIM), LATENT ** -0.5, 0.25, ((0, 8),)),
        "w_o": noise(arg_keys[4], (HEADS * VDIM, D), (HEADS * VDIM) ** -0.5, 0.0625, ((0, 8),)),
        "latent_cache": draw_latent_cache(jax.random.fold_in(arg_keys[7], 71), 0),
        "group_start": jax.random.randint(arg_keys[6], (1,), CACHE // 4, CACHE - GROUP + 1).astype(jnp.int32),
    }


masked_score = -1.0e30


def score_scale():
    return (NOPE + ROPE) ** -0.5 * (0.1 * math.log(32.0) + 1.0) ** 2


def reference(q_nope, q_rope, w_uk, w_uv, w_o, latent_cache, group_start):
    nope_part = q_nope.reshape(GROUP, HEADS, NOPE).astype(jnp.float32)
    latent_query = jnp.einsum("thn,hnl->thl", nope_part, w_uk.astype(jnp.float32)).astype(jnp.bfloat16)
    queries = jnp.concatenate([latent_query, q_rope.reshape(GROUP, HEADS, ROPE)], axis=2)
    query_position = group_start[0] + jnp.arange(GROUP, dtype=jnp.int32)
    visible = jnp.arange(CACHE, dtype=jnp.int32)[None, :] <= query_position[:, None]
    values_part = latent_cache[:LATENT]

    def one_head(inputs):
        head_query, head_uv = inputs
        scores = jnp.dot(head_query, latent_cache, preferred_element_type=jnp.float32) * score_scale()
        scores = jnp.where(visible, scores, masked_score)
        row_best = jnp.max(scores, axis=1)
        weights = jnp.where(visible, jnp.exp(scores - row_best[:, None]), 0.0)
        totals = jnp.sum(weights, axis=1)
        numerator = lax.dot_general(weights.astype(jnp.bfloat16), values_part, (((1,), (1,)), ((), ())), preferred_element_type=jnp.float32)
        latent_out = numerator / totals[:, None]
        return jnp.dot(latent_out, head_uv.astype(jnp.float32), precision=lax.Precision.HIGHEST)

    per_head = lax.map(one_head, (jnp.transpose(queries, (1, 0, 2)), w_uv))
    head_values = jnp.transpose(per_head, (1, 0, 2)).reshape(GROUP, HEADS * VDIM).astype(jnp.bfloat16)
    return jnp.dot(head_values, w_o, preferred_element_type=jnp.float32).astype(jnp.bfloat16)
```

```python
import functools
import math

import jax
import jax.numpy as jnp
from jax import lax
from jax.experimental import pallas as pl
from jax.experimental.pallas import tpu as pltpu
from jax.sharding import PartitionSpec as P

LATENT = 512
ROPE = 64
NOPE = 128
VDIM = 128
HALF = 4
SLOTS = 1024
TOK = 64
PIECE = 2 * TOK
ROWS = PIECE + 16
STEP = 256

F32 = jnp.float32
BF16 = jnp.bfloat16
MASKED = -1e30
SCALE2 = (NOPE + ROPE) ** (-0.5) * (0.1 * math.log(32.0) + 1.0) ** 2 * math.log2(math.e)
VMEM = 56 << 20

CORE = [(i, i ^ 1) for i in range(16)]
ZLO = [(i, i ^ 2) for i in range(16)]
YP = [(i, (i + 4) % 16) for i in range(16)]
YM = [(i, (i - 4) % 16) for i in range(16)]
Y2 = [(i, (i + 8) % 16) for i in range(16)]
XP = [(i, (i // 4) * 4 + (i + 1) % 4) for i in range(8)]
XM = [(i, (i // 4) * 4 + (i - 1) % 4) for i in range(8)]
X2 = [(i, (i // 4) * 4 + (i + 2) % 4) for i in range(8)]
ZHI = [(i, i ^ 4) for i in range(8)]


def to_ctx(array, pairs):
    return lax.ppermute(array, "ctx", pairs)


def to_head(array, pairs):
    return lax.ppermute(array, "head", pairs)


def keys_values_kernel(where_ref, cache_ref, uk_ref, uv_ref, key_ref, val_ref):
    latent = cache_ref[:LATENT]
    rope = cache_ref[LATENT:]
    uk = uk_ref[...].reshape(HALF * NOPE, LATENT)
    keys = jnp.dot(uk, latent, preferred_element_type=F32).astype(BF16)
    uv = jnp.concatenate([uv_ref[h] for h in range(HALF)], axis=1)
    vals = jnp.dot(latent.T, uv, preferred_element_type=F32).astype(BF16)
    blank = jnp.zeros_like(rope)
    ones = jnp.ones((SLOTS, VDIM), BF16)
    for h in range(HALF):
        key_ref[h, :NOPE] = keys[h * NOPE : (h + 1) * NOPE]
        key_ref[h, NOPE : NOPE + ROPE] = rope if h % 2 == 0 else blank
        key_ref[h, NOPE + ROPE :] = blank if h % 2 == 0 else rope
        val_ref[h, :, :VDIM] = vals[:, h * VDIM : (h + 1) * VDIM]
        val_ref[h, :, VDIM:] = ones


def keys_values(where, cache, w_uk, w_uv):
    whole = lambda shape: pl.BlockSpec(shape, lambda i, w: (0,) * len(shape))
    return pl.pallas_call(
        keys_values_kernel,
        grid_spec=pltpu.PrefetchScalarGridSpec(
            num_scalar_prefetch=1,
            grid=(1,),
            in_specs=[
                whole((LATENT + ROPE, SLOTS)),
                pl.BlockSpec((HALF, NOPE, LATENT), lambda i, w: (w[1], 0, 0)),
                pl.BlockSpec((HALF, LATENT, VDIM), lambda i, w: (w[1], 0, 0)),
            ],
            out_specs=[whole((HALF, 256, SLOTS)), whole((HALF, SLOTS, 256))],
        ),
        out_shape=[
            jax.ShapeDtypeStruct((HALF, 256, SLOTS), BF16),
            jax.ShapeDtypeStruct((HALF, SLOTS, 256), BF16),
        ],
        cost_estimate=pl.CostEstimate(
            flops=4 * HALF * NOPE * LATENT * SLOTS, bytes_accessed=6 << 20, transcendentals=0
        ),
        compiler_params=pltpu.CompilerParams(vmem_limit_bytes=VMEM),
        name="keys_values",
    )(where, cache, w_uk, w_uv)


def split3(x):
    a = x.astype(BF16)
    r = x - a.astype(F32)
    b = r.astype(BF16)
    return a, b, (r - b.astype(F32)).astype(BF16)


def store_piece(o_ref, out, lse):
    o_ref[:PIECE] = out.astype(BF16)
    row = lse.T[:1]
    a, b, c = split3(row)
    index = lax.broadcasted_iota(jnp.int32, (16, PIECE), 0)
    spread = lambda v: jnp.broadcast_to(v.astype(F32), (16, PIECE))
    pick = jnp.where(index == 0, spread(a), jnp.where(index == 1, spread(b), jnp.where(index == 2, spread(c), 0.0)))
    o_ref[PIECE:] = pick.astype(BF16)


def attention_kernel(n, where_ref, *refs):
    q_refs, (k0, v0, k1, v1), o_refs = refs[: 2 * n], refs[2 * n : 2 * n + 4], refs[2 * n + 4 :]
    start = where_ref[0]
    core = where_ref[1]
    chip = where_ref[2]
    first = chip * (2 * SLOTS)
    rows = n * PIECE
    q = jnp.concatenate(
        [jnp.concatenate([q_refs[2 * i][...], q_refs[2 * i + 1][...]], axis=1) for i in range(n)], axis=0
    )
    blocks = ((k0, v0, first + core * SLOTS), (k1, v1, first + (1 - core) * SLOTS))

    def positions():
        place = lax.broadcasted_iota(jnp.int32, (PIECE, 1), 0)
        mine = place < TOK
        inner = jnp.where(mine, place, place - TOK)
        side = jnp.where(mine, core, 1 - core)
        local = start + inner + side * TOK
        return jnp.concatenate([local + where_ref[3 + i] * PIECE for i in range(n)], axis=0)

    def scores(k, c):
        return jnp.dot(q, k[0, :, c * STEP : (c + 1) * STEP], preferred_element_type=F32) * SCALE2

    def seen(pos, base, c):
        key = base + c * STEP + lax.broadcasted_iota(jnp.int32, (1, STEP), 1)
        return key <= pos

    def finish(acc, shift):
        total = acc[:, VDIM:]
        none = total == 0.0
        safe = jnp.where(none, 1.0, total)
        out = acc[:, :VDIM] / safe
        lse = jnp.where(none, MASKED, jnp.log2(safe) + shift)
        for i in range(n):
            store_piece(o_refs[i], out[i * PIECE : (i + 1) * PIECE], lse[i * PIECE : (i + 1) * PIECE])

    def quick(masked):
        pos = positions() if masked else None
        acc = None
        for k, v, base in blocks:
            for c in range(SLOTS // STEP):
                p = jnp.exp2(scores(k, c))
                if masked:
                    p = jnp.where(seen(pos, base, c), p, 0.0)
                term = jnp.dot(p.astype(BF16), v[0, c * STEP : (c + 1) * STEP], preferred_element_type=F32)
                acc = term if acc is None else acc + term
        total = acc[:, VDIM:]
        good = (total > 1e-27) & (total < 1e30)
        if masked:
            good = good | (pos < first)
        finish(acc, 0.0)
        return jnp.min(good.astype(F32))

    def careful():
        pos = positions()
        best = jnp.full((rows, 1), MASKED, F32)
        for k, v, base in blocks:
            for c in range(SLOTS // STEP):
                s = jnp.where(seen(pos, base, c), scores(k, c), MASKED)
                best = jnp.maximum(best, jnp.max(s, axis=1, keepdims=True))
        acc = jnp.zeros((rows, 2 * VDIM), F32)
        for k, v, base in blocks:
            for c in range(SLOTS // STEP):
                p = jnp.where(seen(pos, base, c), jnp.exp2(scores(k, c) - best), 0.0)
                acc += jnp.dot(p.astype(BF16), v[0, c * STEP : (c + 1) * STEP], preferred_element_type=F32)
        finish(acc, best)

    everything = first + 2 * SLOTS - 1 <= start
    nothing = first > start + 16 * TOK - 1

    @pl.when(nothing)
    def _():
        for o in o_refs:
            store_piece(o, jnp.zeros((PIECE, VDIM), F32), jnp.full((PIECE, VDIM), MASKED, F32))

    @pl.when(everything)
    def _():
        good = quick(False)

        @pl.when(good < 0.5)
        def _():
            careful()

    @pl.when(jnp.logical_not(everything | nothing))
    def _():
        good = quick(True)

        @pl.when(good < 0.5)
        def _():
            careful()


def attention(where, pieces, own, other):
    n = len(pieces)
    q_specs = []
    q_args = []
    for piece in pieces:
        q_specs += [
            pl.BlockSpec((PIECE, NOPE), lambda h, w: (0, h)),
            pl.BlockSpec((PIECE, 2 * ROPE), lambda h, w: (0, HALF + h // 2)),
        ]
        q_args += [piece, piece]
    kv_specs = [
        pl.BlockSpec((1, 256, SLOTS), lambda h, w: (h, 0, 0)),
        pl.BlockSpec((1, SLOTS, 256), lambda h, w: (h, 0, 0)),
    ] * 2
    return pl.pallas_call(
        functools.partial(attention_kernel, n),
        grid_spec=pltpu.PrefetchScalarGridSpec(
            num_scalar_prefetch=1,
            grid=(HALF,),
            in_specs=q_specs + kv_specs,
            out_specs=[pl.BlockSpec((ROWS, VDIM), lambda h, w: (0, h))] * n,
        ),
        out_shape=[jax.ShapeDtypeStruct((ROWS, HALF * VDIM), BF16)] * n,
        cost_estimate=pl.CostEstimate(
            flops=2 * HALF * n * PIECE * 2 * SLOTS * 512,
            bytes_accessed=8 << 20,
            transcendentals=HALF * n * PIECE * 2 * SLOTS,
        ),
        compiler_params=pltpu.CompilerParams(vmem_limit_bytes=VMEM),
        name="attention",
    )(where, *q_args, *own, *other)


def join_kernel(n, last, *refs):
    pieces, o_ref = refs[:n], refs[n]
    logs = [sum(p[PIECE + j : PIECE + j + 1].astype(F32) for j in range(3)) for p in pieces]
    best = functools.reduce(jnp.maximum, logs)
    shares = [jnp.exp2(v - best) for v in logs]
    total = sum(shares)
    stack = jnp.concatenate([s / total for s in shares] + [best + jnp.log2(total)], axis=0)
    for h in range(HALF):
        lanes = slice(h * VDIM, (h + 1) * VDIM)
        part = stack[:, lanes]
        part = jnp.concatenate([part, jnp.zeros((8 - n - 1, PIECE), F32)], axis=0) if n < 7 else part
        cols = part.T
        out = sum(p[:PIECE, lanes].astype(F32) * cols[:, i : i + 1] for i, p in enumerate(pieces))
        o_ref[:PIECE, lanes] = out.astype(BF16)
    if not last:
        a, b, c = split3(stack[n : n + 1])
        o_ref[PIECE:] = jnp.concatenate(
            [a.astype(F32), b.astype(F32), c.astype(F32), jnp.zeros((13, HALF * VDIM), F32)], axis=0
        ).astype(BF16)


def join(pieces, last=False):
    n = len(pieces)
    width = HALF * VDIM
    rows = PIECE if last else ROWS
    return pl.pallas_call(
        functools.partial(join_kernel, n, last),
        grid=(1,),
        in_specs=[pl.BlockSpec((ROWS, width), lambda i, b=b: (b, 0)) for _, b in pieces],
        out_specs=pl.BlockSpec((rows, width), lambda i: (0, 0)),
        out_shape=jax.ShapeDtypeStruct((rows, width), BF16),
        cost_estimate=pl.CostEstimate(flops=1 << 20, bytes_accessed=1 << 20, transcendentals=4096),
        name="join",
    )(*[a for a, _ in pieces])


def project_kernel(where_ref, mine_ref, theirs_ref, top_ref, low_ref, o_ref):
    acc = jnp.dot(mine_ref[...], top_ref[...], preferred_element_type=F32)
    acc += jnp.dot(theirs_ref[...], low_ref[...], preferred_element_type=F32)
    o_ref[...] = acc.astype(BF16)


def project(where, mine, theirs, w_o, step):
    wide = w_o.shape[1] // 8
    width = HALF * VDIM

    def column(j, w):
        return jnp.where(j == 0, w[8], 1 - w[8]) * 4 + (w[7] + step) % 4

    return pl.pallas_call(
        project_kernel,
        grid_spec=pltpu.PrefetchScalarGridSpec(
            num_scalar_prefetch=1,
            grid=(2,),
            in_specs=[
                pl.BlockSpec((TOK, width), lambda j, w: (0, 0)),
                pl.BlockSpec((TOK, width), lambda j, w: (0, 0)),
                pl.BlockSpec((width, wide), lambda j, w: (w[1], column(j, w))),
                pl.BlockSpec((width, wide), lambda j, w: (1 - w[1], column(j, w))),
            ],
            out_specs=pl.BlockSpec((TOK, wide), lambda j, w: (j, 0)),
        ),
        out_shape=jax.ShapeDtypeStruct((2 * TOK, wide), BF16),
        cost_estimate=pl.CostEstimate(
            flops=2 * 2 * 256 * wide * 1024, bytes_accessed=4 << 20, transcendentals=0
        ),
        name="project",
    )(where, mine, theirs, w_o, w_o)


def on_device(q_nope, q_rope, w_uk, w_uv, w_o, latent_cache, group_start):
    ctx = lax.axis_index("ctx")
    head = lax.axis_index("head")
    core = ctx % 2
    chip = ctx // 2
    y = chip // 2
    z = chip % 2
    place = lambda dy, flip: ((y + dy) % 4) * 2 + (z ^ flip)
    spots = lambda *chips: jnp.stack(
        [group_start[0], core, chip, *chips, head % 4, head // 4]
    ).astype(jnp.int32)
    near = spots(place(0, 0), place(0, 1), place(1, 0), place(3, 0))
    far = spots(place(1, 1), place(3, 1), place(2, 0), place(2, 1))

    def half(side):
        return jnp.concatenate(
            [
                lax.dynamic_slice_in_dim(q_nope, side * (HALF * NOPE), HALF * NOPE, 1),
                lax.dynamic_slice_in_dim(q_rope, side * (HALF * ROPE), HALF * ROPE, 1),
            ],
            axis=1,
        )

    given = to_ctx(half(1 - core), CORE)
    cache_other = to_ctx(latent_cache, CORE)
    u = jnp.concatenate([half(core), given], axis=0)
    w = to_ctx(u, ZLO)
    d_u = to_ctx(u, Y2)
    m_u = to_ctx(u, YP)
    p_u = to_ctx(u, YM)
    m_w = to_ctx(w, YP)
    p_w = to_ctx(w, YM)
    d_w = to_ctx(d_u, ZLO)

    own = keys_values(near, latent_cache, w_uk, w_uv)
    other = keys_values(near, cache_other, w_uk, w_uv)
    r_u, r_w, r_pu, r_mu = attention(near, [u, w, p_u, m_u], own, other)
    r_pw, r_mw, r_du, r_dw = attention(far, [p_w, m_w, d_u, d_w], own, other)

    across = to_ctx(r_dw, ZLO)
    from_d = to_ctx(join([(r_du, 0), (across, 0)]), Y2)
    from_m = to_ctx(jnp.concatenate([r_pu, r_pw], axis=0), YP)
    from_p = to_ctx(jnp.concatenate([r_mu, r_mw], axis=0), YM)
    from_z = to_ctx(join([(r_w, 0), (from_m, 1), (from_p, 1)]), ZLO)
    values = join([(r_u, 0), (from_m, 0), (from_p, 0), (from_d, 0), (from_z, 0)], last=True)

    theirs = to_ctx(values[TOK:], CORE)
    mine = values[:TOK]
    out2 = to_head(project(near, mine, theirs, w_o, 2), X2)
    out1 = to_head(project(near, mine, theirs, w_o, 1), XP)
    out3 = to_head(project(near, mine, theirs, w_o, 3), XM)
    out0 = project(near, mine, theirs, w_o, 0)
    total = out0.astype(F32) + out1.astype(F32) + out2.astype(F32) + out3.astype(F32)
    back = to_head(total[TOK:].astype(BF16), ZHI)
    return (total[:TOK] + back.astype(F32)).astype(BF16)


def solution(mesh):
    placed = (
        P("ctx", "head"),
        P("ctx", "head"),
        P("head", None, None),
        P("head", None, None),
        P("head", None),
        P(None, "ctx"),
        P(),
    )
    return jax.shard_map(
        on_device, mesh=mesh, in_specs=placed, out_specs=P("ctx", "head"), check_vma=False
    )
```

```python
import functools
import math

import jax
import jax.numpy as jnp
from jax import lax
from jax.experimental import pallas as pl
from jax.experimental.pallas import tpu as pltpu
from jax.sharding import PartitionSpec as P

LATENT = 512
ROPE = 64
NOPE = 128
VDIM = 128
HALF = 4
SLOTS = 1024
TOK = 64
PIECE = 2 * TOK
ROWS = PIECE + 16
STEP = 256

F32 = jnp.float32
BF16 = jnp.bfloat16
MASKED = -1e30
SCALE2 = (NOPE + ROPE) ** (-0.5) * (0.1 * math.log(32.0) + 1.0) ** 2 * math.log2(math.e)
VMEM = 20 << 20

CORE = [(i, i ^ 1) for i in range(16)]
ZLO = [(i, i ^ 2) for i in range(16)]
YP = [(i, (i + 4) % 16) for i in range(16)]
YM = [(i, (i - 4) % 16) for i in range(16)]
Y2 = [(i, (i + 8) % 16) for i in range(16)]
DIAGP = [(i, (i + 4) % 16 ^ 2) for i in range(16)]
DIAGM = [(i, (i - 4) % 16 ^ 2) for i in range(16)]
DIAG2 = [(i, (i + 8) % 16 ^ 2) for i in range(16)]
XP = [(i, (i // 4) * 4 + (i + 1) % 4) for i in range(8)]
XM = [(i, (i // 4) * 4 + (i - 1) % 4) for i in range(8)]
X2 = [(i, (i // 4) * 4 + (i + 2) % 4) for i in range(8)]
ZHI = [(i, i ^ 4) for i in range(8)]


def to_ctx(array, pairs):
    return lax.ppermute(array, "ctx", pairs)


def to_head(array, pairs):
    return lax.ppermute(array, "head", pairs)


def vmem(n):
    return [pl.BlockSpec(memory_space=pltpu.VMEM)] * n


SMEM = pl.BlockSpec(memory_space=pltpu.SMEM)
HBM = pl.BlockSpec(memory_space=pltpu.HBM)


def lanes(index, width=128):
    return pl.ds(pl.multiple_of(index * width, 128), width)


def split_kernel(nope_ref, rope_ref, keep_ref, give_ref, sems):
    core = lax.axis_index("ctx") & 1
    copies = []
    for ref, side in ((give_ref, 1 - core), (keep_ref, core)):
        for source, target in (
            (nope_ref.at[:, lanes(side, HALF * NOPE)], ref.at[:, : HALF * NOPE]),
            (rope_ref.at[:, lanes(side, HALF * ROPE)], ref.at[:, HALF * NOPE :]),
        ):
            copies.append(pltpu.make_async_copy(source, target, sems.at[len(copies)]))
    for copy in copies:
        copy.start()
    for copy in copies:
        copy.wait()


def split_queries(q_nope, q_rope):
    shape = jax.ShapeDtypeStruct((TOK, HALF * (NOPE + ROPE)), BF16)
    return pl.pallas_call(
        split_kernel,
        in_specs=[HBM] * 2,
        out_specs=vmem(2),
        out_shape=[shape, shape],
        scratch_shapes=[pltpu.SemaphoreType.DMA((4,))],
        compiler_params=pltpu.CompilerParams(vmem_limit_bytes=4 << 20),
        name="split_queries",
    )(q_nope, q_rope)


def form(cache, uk, uv, key_ref, val_ref):
    slots = cache.shape[1]
    latent = cache[:LATENT]
    rope = cache[LATENT:]
    blank = jnp.zeros((ROPE, slots), BF16)
    ones = jnp.ones((slots, VDIM), BF16)
    keys = jnp.dot(uk[...].reshape(HALF * NOPE, LATENT), latent, preferred_element_type=F32).astype(BF16)
    up = jnp.concatenate([uv[h] for h in range(HALF)], axis=1)
    vals = jnp.dot(latent.T, up, preferred_element_type=F32).astype(BF16)
    for h in range(HALF):
        key_ref[h, :NOPE] = keys[h * NOPE : (h + 1) * NOPE]
        key_ref[h, NOPE : NOPE + ROPE] = rope if h % 2 == 0 else blank
        key_ref[h, NOPE + ROPE :] = blank if h % 2 == 0 else rope
        val_ref[h, :, :VDIM] = vals[:, h * VDIM : (h + 1) * VDIM]
        val_ref[h, :, VDIM:] = ones


def near_kernel(cache_ref, other_ref, uk_ref, uv_ref, key0, val0, key1, val1, uk, uv, own, sems):
    heads = pl.ds((lax.axis_index("ctx") & 1) * HALF, HALF)
    copies = [
        pltpu.make_async_copy(source, target, sems.at[i])
        for i, (source, target) in enumerate(((uk_ref.at[heads], uk), (uv_ref.at[heads], uv), (cache_ref, own)))
    ]
    for copy in copies:
        copy.start()
    copies[0].wait()
    copies[1].wait()
    form(other_ref, uk, uv, key1, val1)
    copies[2].wait()
    form(own, uk, uv, key0, val0)


def kv_shapes(slots):
    return [jax.ShapeDtypeStruct((HALF, 256, slots), BF16), jax.ShapeDtypeStruct((HALF, slots, 256), BF16)]


def kv_cost(slots):
    return pl.CostEstimate(flops=4 * HALF * NOPE * LATENT * slots, bytes_accessed=4 << 20, transcendentals=0)


def near_keys_values(cache, other, w_uk, w_uv):
    uk = jax.ShapeDtypeStruct((HALF, NOPE, LATENT), BF16)
    uv = jax.ShapeDtypeStruct((HALF, LATENT, VDIM), BF16)
    return pl.pallas_call(
        near_kernel,
        in_specs=[HBM] + vmem(1) + [HBM] * 2,
        out_specs=vmem(6),
        out_shape=kv_shapes(SLOTS) * 2 + [uk, uv],
        scratch_shapes=[pltpu.VMEM((LATENT + ROPE, SLOTS), BF16), pltpu.SemaphoreType.DMA((3,))],
        cost_estimate=kv_cost(2 * SLOTS),
        compiler_params=pltpu.CompilerParams(vmem_limit_bytes=12 << 20),
        name="near_keys_values",
    )(cache, other, w_uk, w_uv)


def far_keys_values(cache, uk, uv):
    slots = cache.shape[1]
    return pl.pallas_call(
        form,
        in_specs=vmem(3),
        out_specs=vmem(2),
        out_shape=kv_shapes(slots),
        cost_estimate=kv_cost(slots),
        compiler_params=pltpu.CompilerParams(vmem_limit_bytes=12 << 20),
        name="far_keys_values",
    )(cache, uk, uv)


def split3(x):
    a = x.astype(BF16)
    r = x - a.astype(F32)
    b = r.astype(BF16)
    return a, b, (r - b.astype(F32)).astype(BF16)


def store_piece(o_ref, h, out, lse):
    o_ref[:PIECE, lanes(h)] = out.astype(BF16)
    row = lse.T[:1]
    a, b, c = split3(row)
    index = lax.broadcasted_iota(jnp.int32, (16, PIECE), 0)
    spread = lambda v: jnp.broadcast_to(v.astype(F32), (16, PIECE))
    pick = jnp.where(index == 0, spread(a), jnp.where(index == 1, spread(b), jnp.where(index == 2, spread(c), 0.0)))
    o_ref[PIECE:, lanes(h)] = pick.astype(BF16)


def attention_kernel(places, carried, last, bases, spot_ref, *refs):
    n = len(places)
    rows = n * PIECE
    m = n + 2 * len(bases)
    q_refs, kv_refs, refs = refs[:n], refs[n:m], refs[m:]
    carry, o_refs = (refs[:2], refs[2:]) if carried else (None, refs)
    start = spot_ref[0]
    core = spot_ref[1]
    slots = kv_refs[0].shape[2]
    blocks = [(kv_refs[2 * i], kv_refs[2 * i + 1], spot_ref[b] * SLOTS) for i, b in enumerate(bases)]
    first = functools.reduce(jnp.minimum, [b for _, _, b in blocks])
    final = functools.reduce(jnp.maximum, [b for _, _, b in blocks]) + slots - 1

    def queries(h):
        tall = lambda lane: jnp.concatenate([q[:, lane] for q in q_refs], axis=0)
        return jnp.concatenate([tall(lanes(h)), tall(lanes(HALF + h // 2))], axis=1)

    def positions():
        place = lax.broadcasted_iota(jnp.int32, (PIECE, 1), 0)
        mine = place < TOK
        inner = jnp.where(mine, place, place - TOK)
        side = jnp.where(mine, core, 1 - core)
        local = start + inner + side * TOK
        return jnp.concatenate([local + spot_ref[i] * PIECE for i in places], axis=0)

    def scores(q, k, h, c):
        return jnp.dot(q, k[h, :, c * STEP : (c + 1) * STEP], preferred_element_type=F32) * SCALE2

    def seen(pos, base, c):
        key = base + c * STEP + lax.broadcasted_iota(jnp.int32, (1, STEP), 1)
        return key <= pos

    def finish(h, acc, shift):
        if carried:
            old, old_shift = carry[0][h], carry[1][h]
            shift = jnp.where(acc[:, VDIM:] == 0.0, MASKED, shift)
            best = jnp.maximum(shift, old_shift)
            new_part, old_part = jnp.exp2(shift - best), jnp.exp2(old_shift - best)
            out = acc[:, :VDIM] * new_part + old[:, :VDIM] * old_part
            total = acc[:, VDIM:] * new_part + old[:, VDIM:] * old_part
            shift = best
        else:
            out, total = acc[:, :VDIM], acc[:, VDIM:]
            shift = jnp.where(total == 0.0, MASKED, shift)
        if not last:
            o_refs[0][h, :, :VDIM] = out
            o_refs[0][h, :, VDIM:] = total
            o_refs[1][h] = shift
            return
        none = total == 0.0
        safe = jnp.where(none, 1.0, total)
        out = out / safe
        lse = jnp.where(none, MASKED, jnp.log2(safe) + shift)
        for i in range(n):
            store_piece(o_refs[i], h, out[i * PIECE : (i + 1) * PIECE], lse[i * PIECE : (i + 1) * PIECE])

    def quick(masked):
        pos = positions() if masked else None

        def one(h, fine):
            q = queries(h)
            acc = None
            for k, v, base in blocks:
                for c in range(slots // STEP):
                    p = jnp.exp2(scores(q, k, h, c))
                    if masked:
                        p = jnp.where(seen(pos, base, c), p, 0.0)
                    term = jnp.dot(p.astype(BF16), v[h, c * STEP : (c + 1) * STEP], preferred_element_type=F32)
                    acc = term if acc is None else acc + term
            total = acc[:, VDIM:]
            good = (total > 1e-27) & (total < 1e30)
            if masked:
                good = good | (pos < first)
            finish(h, acc, 0.0)
            return jnp.minimum(fine, good.astype(F32).reshape(rows // 8, 8, VDIM).min(axis=0))

        return jnp.min(lax.fori_loop(0, HALF, one, jnp.ones((8, VDIM), F32)))

    def careful():
        pos = positions()

        def one(h, _):
            q = queries(h)
            best = jnp.full((rows, 1), MASKED, F32)
            for k, v, base in blocks:
                for c in range(slots // STEP):
                    s = jnp.where(seen(pos, base, c), scores(q, k, h, c), MASKED)
                    best = jnp.maximum(best, jnp.max(s, axis=1, keepdims=True))
            acc = jnp.zeros((rows, 2 * VDIM), F32)
            for k, v, base in blocks:
                for c in range(slots // STEP):
                    p = jnp.where(seen(pos, base, c), jnp.exp2(scores(q, k, h, c) - best), 0.0)
                    acc += jnp.dot(p.astype(BF16), v[h, c * STEP : (c + 1) * STEP], preferred_element_type=F32)
            finish(h, acc, best)
            return 0

        lax.fori_loop(0, HALF, one, 0)

    everything = final <= start
    nothing = first > start + 16 * TOK - 1

    @pl.when(nothing)
    def _():
        def one(h, _):
            finish(h, jnp.zeros((rows, 2 * VDIM), F32), MASKED)
            return 0

        lax.fori_loop(0, HALF, one, 0)

    @pl.when(everything)
    def _():
        good = quick(False)

        @pl.when(good < 0.5)
        def _():
            careful()

    @pl.when(jnp.logical_not(everything | nothing))
    def _():
        good = quick(True)

        @pl.when(good < 0.5)
        def _():
            careful()


def attention(spot, places, pieces, keys_vals, bases, carry=(), last=False):
    n = len(pieces)
    slots = keys_vals[0].shape[2]
    if last:
        shapes = [jax.ShapeDtypeStruct((ROWS, HALF * VDIM), BF16)] * n
    else:
        shapes = [
            jax.ShapeDtypeStruct((HALF, n * PIECE, 2 * VDIM), F32),
            jax.ShapeDtypeStruct((HALF, n * PIECE, VDIM), F32),
        ]
    return pl.pallas_call(
        functools.partial(attention_kernel, places, len(carry) > 0, last, bases),
        in_specs=[SMEM] + vmem(n + len(keys_vals) + len(carry)),
        out_specs=vmem(len(shapes)),
        out_shape=shapes,
        cost_estimate=pl.CostEstimate(
            flops=len(keys_vals) * HALF * n * PIECE * slots * 512,
            bytes_accessed=4 << 20,
            transcendentals=HALF * n * PIECE * 2 * slots,
        ),
        compiler_params=pltpu.CompilerParams(vmem_limit_bytes=VMEM),
        name="attention",
    )(spot, *pieces, *keys_vals, *carry)


def join_kernel(n, *refs):
    pieces, o_ref = refs[:n], refs[n]
    logs = [sum(p[PIECE + j : PIECE + j + 1].astype(F32) for j in range(3)) for p in pieces]
    best = functools.reduce(jnp.maximum, logs)
    shares = [jnp.exp2(v - best) for v in logs]
    total = sum(shares)
    stack = jnp.concatenate([s / total for s in shares] + [jnp.zeros((-n % 8, HALF * VDIM), F32)][: -n % 8], axis=0)
    for h in range(HALF):
        lane = slice(h * VDIM, (h + 1) * VDIM)
        cols = stack[:, lane].T
        out = sum(p[:PIECE, lane].astype(F32) * cols[:, i : i + 1] for i, p in enumerate(pieces))
        o_ref[:, lane] = out.astype(BF16)


def join(pieces):
    n = len(pieces)
    return pl.pallas_call(
        functools.partial(join_kernel, n),
        in_specs=vmem(n),
        out_specs=vmem(1)[0],
        out_shape=jax.ShapeDtypeStruct((PIECE, HALF * VDIM), BF16),
        cost_estimate=pl.CostEstimate(flops=1 << 20, bytes_accessed=1 << 20, transcendentals=4096),
        compiler_params=pltpu.CompilerParams(vmem_limit_bytes=8 << 20),
        name="join",
    )(*pieces)


def project_kernel(step, spot_ref, mine_ref, theirs_ref, w_ref, o_ref):
    core, x, zhi = spot_ref[1], spot_ref[3], spot_ref[4]
    wide = o_ref.shape[1]
    rows = HALF * VDIM
    top = pl.ds(pl.multiple_of(core * rows, rows), rows)
    low = pl.ds(pl.multiple_of((1 - core) * rows, rows), rows)
    for j, side in enumerate((zhi, 1 - zhi)):
        column = lanes(side * 4 + ((x + step) & 3), wide)
        acc = jnp.dot(mine_ref[:TOK], w_ref[top, column], preferred_element_type=F32)
        acc += jnp.dot(theirs_ref[...], w_ref[low, column], preferred_element_type=F32)
        o_ref[j * TOK : (j + 1) * TOK] = acc.astype(BF16)


def project(spot, mine, theirs, w_o, step):
    wide = w_o.shape[1] // 8
    return pl.pallas_call(
        functools.partial(project_kernel, step),
        in_specs=[SMEM] + vmem(3),
        out_specs=vmem(1)[0],
        out_shape=jax.ShapeDtypeStruct((2 * TOK, wide), BF16),
        cost_estimate=pl.CostEstimate(
            flops=2 * 2 * 256 * wide * 1024, bytes_accessed=4 << 20, transcendentals=0
        ),
        compiler_params=pltpu.CompilerParams(vmem_limit_bytes=12 << 20),
        name="project",
    )(spot, mine, theirs, w_o)


def on_device(q_nope, q_rope, w_uk, w_uv, w_o, latent_cache, group_start):
    ctx = lax.axis_index("ctx")
    head = lax.axis_index("head")
    chip = ctx >> 1
    place = lambda dy: (((chip >> 1) + dy) & 3) * 2 + (chip & 1)
    spot = jnp.stack(
        [group_start[0], ctx & 1, chip, head & 3, head >> 2]
        + [place(dy) for dy in range(4)]
        + [ctx ^ flip for flip in range(4)]
    ).astype(jnp.int32)
    U, PU, DU, MU = range(5, 9)
    OWN, CORES, ZNEAR, ZCORES = range(9, 13)
    z_cache = to_ctx(latent_cache, ZLO)
    cache_other = to_ctx(latent_cache, CORE)
    keep, give = split_queries(q_nope, q_rope)
    given = to_ctx(give, CORE)
    u = jnp.concatenate([keep, given], axis=0)
    d_u = to_ctx(u, Y2)
    p_u = to_ctx(u, YM)
    m_u = to_ctx(u, YP)

    places, pieces = (U, PU, DU, MU), (u, p_u, d_u, m_u)
    cache_other, u_ = lax.optimization_barrier((cache_other, u))
    *near, uk, uv = near_keys_values(latent_cache, cache_other, w_uk, w_uv)
    carry = attention(spot, places, pieces, near, (OWN, CORES))
    z_cache, carry = lax.optimization_barrier((z_cache, carry))
    zc_cache = to_ctx(z_cache, CORE)
    carry = attention(spot, places, pieces, far_keys_values(z_cache, uk, uv), (ZNEAR,), carry)
    zc_cache, carry = lax.optimization_barrier((zc_cache, carry))
    r_u, r_p, r_d, r_m = attention(
        spot, places, pieces, far_keys_values(zc_cache, uk, uv), (ZCORES,), carry, True
    )
    mine = join([r_u, to_ctx(r_d, Y2), to_ctx(r_p, YP), to_ctx(r_m, YM)])

    theirs = to_ctx(mine[TOK:], CORE)
    out2 = to_head(project(spot, mine, theirs, w_o, 2), X2)
    out1 = to_head(project(spot, mine, theirs, w_o, 1), XP)
    out3 = to_head(project(spot, mine, theirs, w_o, 3), XM)
    out0 = project(spot, mine, theirs, w_o, 0)
    total = out0.astype(F32) + out1.astype(F32) + out2.astype(F32) + out3.astype(F32)
    back = to_head(total[TOK:].astype(BF16), ZHI)
    return (total[:TOK] + back.astype(F32)).astype(BF16)


def solution(mesh):
    placed = (
        P("ctx", "head"),
        P("ctx", "head"),
        P("head", None, None),
        P("head", None, None),
        P("head", None),
        P(None, "ctx"),
        P(),
    )
    return jax.shard_map(
        on_device, mesh=mesh, in_specs=placed, out_specs=P("ctx", "head"), check_vma=False
    )
```

```python
import functools
import math

import jax
import jax.numpy as jnp
from jax import lax
from jax.experimental import pallas as pl
from jax.experimental.pallas import tpu as pltpu
from jax.sharding import PartitionSpec as P

LATENT = 512
ROPE = 64
NOPE = 128
VDIM = 128
HALF = 4
SLOTS = 1024
TOK = 64
PIECE = 2 * TOK
ROWS = PIECE + 16
STEP = 256
PART = SLOTS // 2
SHARE = (SLOTS - PART) // 4

F32 = jnp.float32
BF16 = jnp.bfloat16
MASKED = -1e30
SCALE2 = (NOPE + ROPE) ** (-0.5) * (0.1 * math.log(32.0) + 1.0) ** 2 * math.log2(math.e)
VMEM = 20 << 20

CORE = [(i, i ^ 1) for i in range(16)]
ZLO = [(i, i ^ 2) for i in range(16)]
YP = [(i, (i + 4) % 16) for i in range(16)]
YM = [(i, (i - 4) % 16) for i in range(16)]
Y2 = [(i, (i + 8) % 16) for i in range(16)]
DIAGP = [(i, (i + 4) % 16 ^ 2) for i in range(16)]
DIAGM = [(i, (i - 4) % 16 ^ 2) for i in range(16)]
DIAG2 = [(i, (i + 8) % 16 ^ 2) for i in range(16)]
XP = [(i, (i // 4) * 4 + (i + 1) % 4) for i in range(8)]
XM = [(i, (i // 4) * 4 + (i - 1) % 4) for i in range(8)]
X2 = [(i, (i // 4) * 4 + (i + 2) % 4) for i in range(8)]
ZHI = [(i, i ^ 4) for i in range(8)]


def to_ctx(array, pairs):
    return lax.ppermute(array, "ctx", pairs)


def to_head(array, pairs):
    return lax.ppermute(array, "head", pairs)


def vmem(n):
    return [pl.BlockSpec(memory_space=pltpu.VMEM)] * n


SMEM = pl.BlockSpec(memory_space=pltpu.SMEM)
HBM = pl.BlockSpec(memory_space=pltpu.HBM)


def hbm(x):
    return pltpu.with_memory_space_constraint(x, pltpu.HBM)


def lanes(index, width=128):
    return pl.ds(pl.multiple_of(index * width, 128), width)


def split_kernel(nope_ref, rope_ref, cache_ref, keep_ref, give_ref, half_ref, share_ref, sems):
    core = lax.axis_index("ctx") & 1
    x = lax.axis_index("head") & 3
    copies = []
    for ref, side in ((give_ref, 1 - core), (keep_ref, core)):
        for source, target in (
            (nope_ref.at[:, lanes(side, HALF * NOPE)], ref.at[:, : HALF * NOPE]),
            (rope_ref.at[:, lanes(side, HALF * ROPE)], ref.at[:, HALF * NOPE :]),
        ):
            copies.append(pltpu.make_async_copy(source, target, sems.at[len(copies)]))
    mine = pl.ds(pl.multiple_of(PART + x * SHARE, SHARE), SHARE)
    for source, target in ((cache_ref.at[:, mine], share_ref), (cache_ref.at[:, :PART], half_ref)):
        copies.append(pltpu.make_async_copy(source, target, sems.at[len(copies)]))
    for copy in copies:
        copy.start()
    for copy in copies:
        copy.wait()


def split_queries(q_nope, q_rope, cache):
    shape = jax.ShapeDtypeStruct((TOK, HALF * (NOPE + ROPE)), BF16)
    return pl.pallas_call(
        split_kernel,
        in_specs=[HBM] * 3,
        out_specs=vmem(4),
        out_shape=[shape, shape] + [jax.ShapeDtypeStruct((LATENT + ROPE, n), BF16) for n in (PART, SHARE)],
        scratch_shapes=[pltpu.SemaphoreType.DMA((6,))],
        compiler_params=pltpu.CompilerParams(vmem_limit_bytes=4 << 20),
        name="split_queries",
    )(hbm(q_nope), hbm(q_rope), hbm(cache))


def form(cache, uk, uv, key_ref, val_ref):
    slots = cache.shape[1]
    latent = cache[:LATENT]
    rope = cache[LATENT:]
    blank = jnp.zeros((ROPE, slots), BF16)
    ones = jnp.ones((slots, VDIM), BF16)
    keys = jnp.dot(uk[...].reshape(HALF * NOPE, LATENT), latent, preferred_element_type=F32).astype(BF16)
    up = jnp.concatenate([uv[h] for h in range(HALF)], axis=1)
    vals = jnp.dot(latent.T, up, preferred_element_type=F32).astype(BF16)
    for h in range(HALF):
        key_ref[h, :NOPE] = keys[h * NOPE : (h + 1) * NOPE]
        key_ref[h, NOPE : NOPE + ROPE] = rope if h % 2 == 0 else blank
        key_ref[h, NOPE + ROPE :] = blank if h % 2 == 0 else rope
        val_ref[h, :, :VDIM] = vals[:, h * VDIM : (h + 1) * VDIM]
        val_ref[h, :, VDIM:] = ones


def near_kernel(cache_ref, other_ref, uk_ref, uv_ref, key0, val0, key1, val1, uk, uv, own, sems):
    heads = pl.ds((lax.axis_index("ctx") & 1) * HALF, HALF)
    copies = [
        pltpu.make_async_copy(source, target, sems.at[i])
        for i, (source, target) in enumerate(((uk_ref.at[heads], uk), (uv_ref.at[heads], uv), (cache_ref, own)))
    ]
    for copy in copies:
        copy.start()
    copies[0].wait()
    copies[1].wait()
    form(other_ref, uk, uv, key1, val1)
    copies[2].wait()
    form(own, uk, uv, key0, val0)


def kv_shapes(slots):
    return [jax.ShapeDtypeStruct((HALF, 256, slots), BF16), jax.ShapeDtypeStruct((HALF, slots, 256), BF16)]


def kv_cost(slots):
    return pl.CostEstimate(flops=4 * HALF * NOPE * LATENT * slots, bytes_accessed=4 << 20, transcendentals=0)


def near_keys_values(cache, other, w_uk, w_uv):
    uk = jax.ShapeDtypeStruct((HALF, NOPE, LATENT), BF16)
    uv = jax.ShapeDtypeStruct((HALF, LATENT, VDIM), BF16)
    return pl.pallas_call(
        near_kernel,
        in_specs=[HBM] + vmem(1) + [HBM] * 2,
        out_specs=vmem(6),
        out_shape=kv_shapes(SLOTS) * 2 + [uk, uv],
        scratch_shapes=[pltpu.VMEM((LATENT + ROPE, SLOTS), BF16), pltpu.SemaphoreType.DMA((3,))],
        cost_estimate=kv_cost(2 * SLOTS),
        compiler_params=pltpu.CompilerParams(vmem_limit_bytes=12 << 20),
        name="near_keys_values",
    )(hbm(cache), other, hbm(w_uk), hbm(w_uv))


def far_keys_values(cache, uk, uv):
    slots = cache.shape[1]
    return pl.pallas_call(
        form,
        in_specs=vmem(3),
        out_specs=vmem(2),
        out_shape=kv_shapes(slots),
        cost_estimate=kv_cost(slots),
        compiler_params=pltpu.CompilerParams(vmem_limit_bytes=12 << 20),
        name="far_keys_values",
    )(cache, uk, uv)


def split3(x):
    a = x.astype(BF16)
    r = x - a.astype(F32)
    b = r.astype(BF16)
    return a, b, (r - b.astype(F32)).astype(BF16)


def store_piece(o_ref, h, out, lse):
    o_ref[:PIECE, lanes(h)] = out.astype(BF16)
    row = lse.T[:1]
    a, b, c = split3(row)
    index = lax.broadcasted_iota(jnp.int32, (16, PIECE), 0)
    spread = lambda v: jnp.broadcast_to(v.astype(F32), (16, PIECE))
    pick = jnp.where(index == 0, spread(a), jnp.where(index == 1, spread(b), jnp.where(index == 2, spread(c), 0.0)))
    o_ref[PIECE:, lanes(h)] = pick.astype(BF16)


def attention_kernel(places, carried, last, bases, mixed, spot_ref, *refs):
    n = len(places)
    rows = n * PIECE
    m = n + 2 * len(bases)
    q_refs, kv_refs, refs = refs[:n], refs[n:m], refs[m:]
    carry, o_refs = (refs[:2], refs[2:]) if carried else (None, refs)
    start = spot_ref[0]
    core = spot_ref[1]
    slots = kv_refs[0].shape[2]
    blocks = [(kv_refs[2 * i], kv_refs[2 * i + 1], spot_ref[b] * SLOTS) for i, b in enumerate(bases)]
    first = functools.reduce(jnp.minimum, [b for _, _, b in blocks])
    final = functools.reduce(jnp.maximum, [b for _, _, b in blocks]) + slots - 1

    def queries(h):
        tall = lambda lane: jnp.concatenate([q[:, lane] for q in q_refs], axis=0)
        return jnp.concatenate([tall(lanes(h)), tall(lanes(HALF + h // 2))], axis=1)

    def positions():
        place = lax.broadcasted_iota(jnp.int32, (PIECE, 1), 0)
        mine = place < TOK
        inner = jnp.where(mine, place, place - TOK)
        side = jnp.where(mine, core, 1 - core)
        local = start + inner + side * TOK
        return jnp.concatenate([local + spot_ref[i] * PIECE for i in places], axis=0)

    def scores(q, k, h, c):
        return jnp.dot(q, k[h, :, c * STEP : (c + 1) * STEP], preferred_element_type=F32) * SCALE2

    def seen(pos, base, c):
        if mixed and c * STEP >= PART:
            place = lax.broadcasted_iota(jnp.int32, (1, SHARE), 1)
            two = [spot_ref[13 + (c * STEP - PART) // SHARE + i] * SHARE for i in range(STEP // SHARE)]
            key = jnp.concatenate([base + PART + at + place for at in two], axis=1)
        else:
            key = base + c * STEP + lax.broadcasted_iota(jnp.int32, (1, STEP), 1)
        return key <= pos

    def finish(h, acc, shift):
        if carried:
            old, old_shift = carry[0][h], carry[1][h]
            shift = jnp.where(acc[:, VDIM:] == 0.0, MASKED, shift)
            best = jnp.maximum(shift, old_shift)
            new_part, old_part = jnp.exp2(shift - best), jnp.exp2(old_shift - best)
            out = acc[:, :VDIM] * new_part + old[:, :VDIM] * old_part
            total = acc[:, VDIM:] * new_part + old[:, VDIM:] * old_part
            shift = best
        else:
            out, total = acc[:, :VDIM], acc[:, VDIM:]
            shift = jnp.where(total == 0.0, MASKED, shift)
        if not last:
            o_refs[0][h, :, :VDIM] = out
            o_refs[0][h, :, VDIM:] = total
            o_refs[1][h] = shift
            return
        none = total == 0.0
        safe = jnp.where(none, 1.0, total)
        out = out / safe
        lse = jnp.where(none, MASKED, jnp.log2(safe) + shift)
        for i in range(n):
            store_piece(o_refs[i], h, out[i * PIECE : (i + 1) * PIECE], lse[i * PIECE : (i + 1) * PIECE])

    def quick(masked):
        pos = positions() if masked else None

        def one(h, fine):
            q = queries(h)
            acc = None
            for k, v, base in blocks:
                wide = slots // STEP if len(blocks) == 1 else 1
                weights = []
                for c in range(slots // STEP):
                    p = jnp.exp2(scores(q, k, h, c))
                    if masked:
                        p = jnp.where(seen(pos, base, c), p, 0.0)
                    weights.append(p.astype(BF16))
                    if len(weights) < wide:
                        continue
                    rows_of_v = v[h, (c + 1 - wide) * STEP : (c + 1) * STEP]
                    term = jnp.dot(jnp.concatenate(weights, axis=1), rows_of_v, preferred_element_type=F32)
                    acc = term if acc is None else acc + term
                    weights = []
            total = acc[:, VDIM:]
            good = (total > 1e-27) & (total < 1e30)
            if masked:
                good = good | (pos < first)
            finish(h, acc, 0.0)
            return jnp.minimum(fine, good.astype(F32).reshape(rows // 8, 8, VDIM).min(axis=0))

        return jnp.min(lax.fori_loop(0, HALF, one, jnp.ones((8, VDIM), F32)))

    def careful():
        pos = positions()

        def one(h, _):
            q = queries(h)
            best = jnp.full((rows, 1), MASKED, F32)
            for k, v, base in blocks:
                for c in range(slots // STEP):
                    s = jnp.where(seen(pos, base, c), scores(q, k, h, c), MASKED)
                    best = jnp.maximum(best, jnp.max(s, axis=1, keepdims=True))
            acc = jnp.zeros((rows, 2 * VDIM), F32)
            for k, v, base in blocks:
                for c in range(slots // STEP):
                    p = jnp.where(seen(pos, base, c), jnp.exp2(scores(q, k, h, c) - best), 0.0)
                    acc += jnp.dot(p.astype(BF16), v[h, c * STEP : (c + 1) * STEP], preferred_element_type=F32)
            finish(h, acc, best)
            return 0

        lax.fori_loop(0, HALF, one, 0)

    everything = final <= start
    nothing = first > start + 16 * TOK - 1

    @pl.when(nothing)
    def _():
        def one(h, _):
            finish(h, jnp.zeros((rows, 2 * VDIM), F32), MASKED)
            return 0

        lax.fori_loop(0, HALF, one, 0)

    @pl.when(everything)
    def _():
        good = quick(False)

        @pl.when(good < 0.5)
        def _():
            careful()

    @pl.when(jnp.logical_not(everything | nothing))
    def _():
        good = quick(True)

        @pl.when(good < 0.5)
        def _():
            careful()


def attention(spot, places, pieces, keys_vals, bases, mixed, carry=(), last=False):
    n = len(pieces)
    slots = keys_vals[0].shape[2]
    if last:
        shapes = [jax.ShapeDtypeStruct((ROWS, HALF * VDIM), BF16)] * n
    else:
        shapes = [
            jax.ShapeDtypeStruct((HALF, n * PIECE, 2 * VDIM), F32),
            jax.ShapeDtypeStruct((HALF, n * PIECE, VDIM), F32),
        ]
    return pl.pallas_call(
        functools.partial(attention_kernel, places, len(carry) > 0, last, bases, mixed),
        in_specs=[SMEM] + vmem(n + len(keys_vals) + len(carry)),
        out_specs=vmem(len(shapes)),
        out_shape=shapes,
        cost_estimate=pl.CostEstimate(
            flops=len(keys_vals) * HALF * n * PIECE * slots * 512,
            bytes_accessed=4 << 20,
            transcendentals=HALF * n * PIECE * 2 * slots,
        ),
        compiler_params=pltpu.CompilerParams(vmem_limit_bytes=VMEM),
        name="attention",
    )(spot, *pieces, *keys_vals, *carry)


def join_kernel(n, *refs):
    pieces, o_ref = refs[:n], refs[n]
    logs = [sum(p[PIECE + j : PIECE + j + 1].astype(F32) for j in range(3)) for p in pieces]
    best = functools.reduce(jnp.maximum, logs)
    shares = [jnp.exp2(v - best) for v in logs]
    total = sum(shares)
    stack = jnp.concatenate([s / total for s in shares] + [jnp.zeros((-n % 8, HALF * VDIM), F32)][: -n % 8], axis=0)
    for h in range(HALF):
        lane = slice(h * VDIM, (h + 1) * VDIM)
        cols = stack[:, lane].T
        out = sum(p[:PIECE, lane].astype(F32) * cols[:, i : i + 1] for i, p in enumerate(pieces))
        o_ref[:, lane] = out.astype(BF16)


def join(pieces):
    n = len(pieces)
    return pl.pallas_call(
        functools.partial(join_kernel, n),
        in_specs=vmem(n),
        out_specs=vmem(1)[0],
        out_shape=jax.ShapeDtypeStruct((PIECE, HALF * VDIM), BF16),
        cost_estimate=pl.CostEstimate(flops=1 << 20, bytes_accessed=1 << 20, transcendentals=4096),
        compiler_params=pltpu.CompilerParams(vmem_limit_bytes=8 << 20),
        name="join",
    )(*pieces)


def project_kernel(step, spot_ref, mine_ref, theirs_ref, w_ref, o_ref):
    core, x, zhi = spot_ref[1], spot_ref[3], spot_ref[4]
    wide = o_ref.shape[1]
    rows = HALF * VDIM
    top = pl.ds(pl.multiple_of(core * rows, rows), rows)
    low = pl.ds(pl.multiple_of((1 - core) * rows, rows), rows)
    for j, side in enumerate((zhi, 1 - zhi)):
        column = lanes(side * 4 + ((x + step) & 3), wide)
        acc = jnp.dot(mine_ref[:TOK], w_ref[top, column], preferred_element_type=F32)
        acc += jnp.dot(theirs_ref[...], w_ref[low, column], preferred_element_type=F32)
        o_ref[j * TOK : (j + 1) * TOK] = acc.astype(BF16)


def project(spot, mine, theirs, w_o, step):
    wide = w_o.shape[1] // 8
    return pl.pallas_call(
        functools.partial(project_kernel, step),
        in_specs=[SMEM] + vmem(3),
        out_specs=vmem(1)[0],
        out_shape=jax.ShapeDtypeStruct((2 * TOK, wide), BF16),
        cost_estimate=pl.CostEstimate(
            flops=2 * 2 * 256 * wide * 1024, bytes_accessed=4 << 20, transcendentals=0
        ),
        compiler_params=pltpu.CompilerParams(vmem_limit_bytes=12 << 20),
        name="project",
    )(spot, mine, theirs, w_o)


def on_device(q_nope, q_rope, w_uk, w_uv, w_o, latent_cache, group_start):
    ctx = lax.axis_index("ctx")
    head = lax.axis_index("head")
    chip = ctx >> 1
    place = lambda dy: (((chip >> 1) + dy) & 3) * 2 + (chip & 1)
    spot = jnp.stack(
        [group_start[0], ctx & 1, chip, head & 3, head >> 2]
        + [place(dy) for dy in range(4)]
        + [ctx ^ flip for flip in range(4)]
        + [(head + step) & 3 for step in (0, 3, 1, 2)]
    ).astype(jnp.int32)
    U, PU, DU, MU = range(5, 9)
    OWN, CORES, ZNEAR, ZCORES = range(9, 13)
    cache_other = to_ctx(latent_cache, CORE)
    keep, give, half, share = split_queries(q_nope, q_rope, latent_cache)
    z_share = to_ctx(share, ZLO)
    given = to_ctx(give, CORE)
    u = jnp.concatenate([keep, given], axis=0)
    d_u = to_ctx(u, Y2)
    p_u = to_ctx(u, YM)
    m_u = to_ctx(u, YP)
    z_share, half = lax.optimization_barrier((z_share, half))
    z_half = to_ctx(half, ZLO)
    near = near_keys_values(latent_cache, cache_other, w_uk, w_uv)
    z_share, near = lax.optimization_barrier((z_share, near))
    *near, uk, uv = near
    shares = [z_share, to_head(z_share, XP), to_head(z_share, XM), to_head(z_share, X2)]

    places, pieces = (U, DU, PU, MU), (u, d_u, p_u, m_u)
    carry = attention(spot, places, pieces, near, (OWN, CORES), False)
    shares, z_half, carry = lax.optimization_barrier((shares, z_half, carry))
    z_cache = jnp.concatenate([z_half] + shares, axis=1)
    zc_cache = to_ctx(z_cache, CORE)
    carry = attention(spot, places, pieces, far_keys_values(z_cache, uk, uv), (ZNEAR,), True, carry)
    zc_cache, carry = lax.optimization_barrier((zc_cache, carry))
    r_u, r_d, r_p, r_m = attention(
        spot, places, pieces, far_keys_values(zc_cache, uk, uv), (ZCORES,), True, carry, True
    )
    mine = join([r_u, to_ctx(r_d, Y2), to_ctx(r_p, YP), to_ctx(r_m, YM)])

    theirs = to_ctx(mine[TOK:], CORE)
    out2 = to_head(project(spot, mine, theirs, w_o, 2), X2)
    out1 = to_head(project(spot, mine, theirs, w_o, 1), XP)
    out3 = to_head(project(spot, mine, theirs, w_o, 3), XM)
    out0 = project(spot, mine, theirs, w_o, 0)
    total = out0.astype(F32) + out1.astype(F32) + out2.astype(F32) + out3.astype(F32)
    back = to_head(total[TOK:].astype(BF16), ZHI)
    return (total[:TOK] + back.astype(F32)).astype(BF16)


def solution(mesh):
    placed = (
        P("ctx", "head"),
        P("ctx", "head"),
        P("head", None, None),
        P("head", None, None),
        P("head", None),
        P(None, "ctx"),
        P(),
    )
    return jax.shard_map(
        on_device, mesh=mesh, in_specs=placed, out_specs=P("ctx", "head"), check_vma=False
    )
```

```python
import functools
import math

import jax
import jax.numpy as jnp
from jax import lax
from jax.experimental import pallas as pl
from jax.experimental.pallas import tpu as pltpu
from jax.sharding import PartitionSpec as P

LATENT = 512
ROPE = 64
NOPE = 128
VDIM = 128
HALF = 4
SLOTS = 1024
TOK = 64
PIECE = 2 * TOK
ROWS = PIECE + 16
STEP = 256
PART = SLOTS // 2
SHARE = (SLOTS - PART) // 2

F32 = jnp.float32
BF16 = jnp.bfloat16
MASKED = -1e30
SCALE2 = (NOPE + ROPE) ** (-0.5) * (0.1 * math.log(32.0) + 1.0) ** 2 * math.log2(math.e)
VMEM = 20 << 20

CORE = [(i, i ^ 1) for i in range(16)]
ZLO = [(i, i ^ 2) for i in range(16)]
YP = [(i, (i + 4) % 16) for i in range(16)]
YM = [(i, (i - 4) % 16) for i in range(16)]
Y2 = [(i, (i + 8) % 16) for i in range(16)]
DIAGP = [(i, (i + 4) % 16 ^ 2) for i in range(16)]
DIAGM = [(i, (i - 4) % 16 ^ 2) for i in range(16)]
DIAG2 = [(i, (i + 8) % 16 ^ 2) for i in range(16)]
XP = [(i, (i // 4) * 4 + (i + 1) % 4) for i in range(8)]
XM = [(i, (i // 4) * 4 + (i - 1) % 4) for i in range(8)]
X2 = [(i, (i // 4) * 4 + (i + 2) % 4) for i in range(8)]
ZHI = [(i, i ^ 4) for i in range(8)]
XSIDE = [(i, i ^ 1) for i in range(8)]


def to_ctx(array, pairs):
    return lax.ppermute(array, "ctx", pairs)


def to_head(array, pairs):
    return lax.ppermute(array, "head", pairs)


def vmem(n):
    return [pl.BlockSpec(memory_space=pltpu.VMEM)] * n


SMEM = pl.BlockSpec(memory_space=pltpu.SMEM)
HBM = pl.BlockSpec(memory_space=pltpu.HBM)


def hbm(x):
    return pltpu.with_memory_space_constraint(x, pltpu.HBM)


def lanes(index, width=128):
    return pl.ds(pl.multiple_of(index * width, 128), width)


def split_kernel(nope_ref, rope_ref, cache_ref, keep_ref, give_ref, half_ref, share_ref, sems):
    core = lax.axis_index("ctx") & 1
    odd = lax.axis_index("head") & 1
    copies = []
    for ref, side in ((give_ref, 1 - core), (keep_ref, core)):
        for source, target in (
            (nope_ref.at[:, lanes(side, HALF * NOPE)], ref.at[:, : HALF * NOPE]),
            (rope_ref.at[:, lanes(side, HALF * ROPE)], ref.at[:, HALF * NOPE :]),
        ):
            copies.append(pltpu.make_async_copy(source, target, sems.at[len(copies)]))
    mine = pl.ds(pl.multiple_of(PART + odd * SHARE, SHARE), SHARE)
    for source, target in ((cache_ref.at[:, mine], share_ref), (cache_ref.at[:, :PART], half_ref)):
        copies.append(pltpu.make_async_copy(source, target, sems.at[len(copies)]))
    for copy in copies:
        copy.start()
    for copy in copies:
        copy.wait()


def split_queries(q_nope, q_rope, cache):
    shape = jax.ShapeDtypeStruct((TOK, HALF * (NOPE + ROPE)), BF16)
    return pl.pallas_call(
        split_kernel,
        in_specs=[HBM] * 3,
        out_specs=vmem(4),
        out_shape=[shape, shape] + [jax.ShapeDtypeStruct((LATENT + ROPE, n), BF16) for n in (PART, SHARE)],
        scratch_shapes=[pltpu.SemaphoreType.DMA((6,))],
        compiler_params=pltpu.CompilerParams(vmem_limit_bytes=4 << 20),
        name="split_queries",
    )(hbm(q_nope), hbm(q_rope), hbm(cache))


def form(cache, uk, uv, key_ref, val_ref):
    slots = cache.shape[1]
    latent = cache[:LATENT]
    rope = cache[LATENT:]
    blank = jnp.zeros((ROPE, slots), BF16)
    ones = jnp.ones((slots, VDIM), BF16)
    keys = jnp.dot(uk[...].reshape(HALF * NOPE, LATENT), latent, preferred_element_type=F32).astype(BF16)
    up = jnp.concatenate([uv[h] for h in range(HALF)], axis=1)
    vals = jnp.dot(latent.T, up, preferred_element_type=F32).astype(BF16)
    for h in range(HALF):
        key_ref[h, :NOPE] = keys[h * NOPE : (h + 1) * NOPE]
        key_ref[h, NOPE : NOPE + ROPE] = rope if h % 2 == 0 else blank
        key_ref[h, NOPE + ROPE :] = blank if h % 2 == 0 else rope
        val_ref[h, :, :VDIM] = vals[:, h * VDIM : (h + 1) * VDIM]
        val_ref[h, :, VDIM:] = ones


def near_kernel(cache_ref, other_ref, uk_ref, uv_ref, key0, val0, key1, val1, uk, uv, own, sems):
    heads = pl.ds((lax.axis_index("ctx") & 1) * HALF, HALF)
    copies = [
        pltpu.make_async_copy(source, target, sems.at[i])
        for i, (source, target) in enumerate(((uk_ref.at[heads], uk), (uv_ref.at[heads], uv), (cache_ref, own)))
    ]
    for copy in copies:
        copy.start()
    copies[0].wait()
    copies[1].wait()
    form(other_ref, uk, uv, key1, val1)
    copies[2].wait()
    form(own, uk, uv, key0, val0)


def kv_shapes(slots):
    return [jax.ShapeDtypeStruct((HALF, 256, slots), BF16), jax.ShapeDtypeStruct((HALF, slots, 256), BF16)]


def kv_cost(slots):
    return pl.CostEstimate(flops=4 * HALF * NOPE * LATENT * slots, bytes_accessed=4 << 20, transcendentals=0)


def near_keys_values(cache, other, w_uk, w_uv):
    uk = jax.ShapeDtypeStruct((HALF, NOPE, LATENT), BF16)
    uv = jax.ShapeDtypeStruct((HALF, LATENT, VDIM), BF16)
    return pl.pallas_call(
        near_kernel,
        in_specs=[HBM] + vmem(1) + [HBM] * 2,
        out_specs=vmem(6),
        out_shape=kv_shapes(SLOTS) * 2 + [uk, uv],
        scratch_shapes=[pltpu.VMEM((LATENT + ROPE, SLOTS), BF16), pltpu.SemaphoreType.DMA((3,))],
        cost_estimate=kv_cost(2 * SLOTS),
        compiler_params=pltpu.CompilerParams(vmem_limit_bytes=12 << 20),
        name="near_keys_values",
    )(hbm(cache), other, hbm(w_uk), hbm(w_uv))


def far_keys_values(cache, uk, uv):
    slots = cache.shape[1]
    return pl.pallas_call(
        form,
        in_specs=vmem(3),
        out_specs=vmem(2),
        out_shape=kv_shapes(slots),
        cost_estimate=kv_cost(slots),
        compiler_params=pltpu.CompilerParams(vmem_limit_bytes=12 << 20),
        name="far_keys_values",
    )(cache, uk, uv)


def split3(x):
    a = x.astype(BF16)
    r = x - a.astype(F32)
    b = r.astype(BF16)
    return a, b, (r - b.astype(F32)).astype(BF16)


def store_piece(o_ref, h, out, lse):
    o_ref[:PIECE, lanes(h)] = out.astype(BF16)
    row = lse.T[:1]
    a, b, c = split3(row)
    index = lax.broadcasted_iota(jnp.int32, (16, PIECE), 0)
    spread = lambda v: jnp.broadcast_to(v.astype(F32), (16, PIECE))
    pick = jnp.where(index == 0, spread(a), jnp.where(index == 1, spread(b), jnp.where(index == 2, spread(c), 0.0)))
    o_ref[PIECE:, lanes(h)] = pick.astype(BF16)


def attention_kernel(places, carried, last, bases, mixed, spot_ref, *refs):
    n = len(places)
    rows = n * PIECE
    m = n + 2 * len(bases)
    q_refs, kv_refs, refs = refs[:n], refs[n:m], refs[m:]
    carry, o_refs = (refs[:2], refs[2:]) if carried else (None, refs)
    start = spot_ref[0]
    core = spot_ref[1]
    slots = kv_refs[0].shape[2]
    blocks = [(kv_refs[2 * i], kv_refs[2 * i + 1], spot_ref[b] * SLOTS) for i, b in enumerate(bases)]
    first = functools.reduce(jnp.minimum, [b for _, _, b in blocks])
    final = functools.reduce(jnp.maximum, [b for _, _, b in blocks]) + slots - 1

    def queries(h):
        tall = lambda lane: jnp.concatenate([q[:, lane] for q in q_refs], axis=0)
        return jnp.concatenate([tall(lanes(h)), tall(lanes(HALF + h // 2))], axis=1)

    def positions():
        place = lax.broadcasted_iota(jnp.int32, (PIECE, 1), 0)
        mine = place < TOK
        inner = jnp.where(mine, place, place - TOK)
        side = jnp.where(mine, core, 1 - core)
        local = start + inner + side * TOK
        return jnp.concatenate([local + spot_ref[i] * PIECE for i in places], axis=0)

    def scores(q, k, h, c):
        return jnp.dot(q, k[h, :, c * STEP : (c + 1) * STEP], preferred_element_type=F32) * SCALE2

    def seen(pos, base, c):
        at = c * STEP
        if mixed and at >= PART:
            at = PART + spot_ref[13 + (at - PART) // SHARE] * SHARE
        key = base + at + lax.broadcasted_iota(jnp.int32, (1, STEP), 1)
        return key <= pos

    def finish(h, acc, shift):
        if carried:
            old, old_shift = carry[0][h], carry[1][h]
            shift = jnp.where(acc[:, VDIM:] == 0.0, MASKED, shift)
            best = jnp.maximum(shift, old_shift)
            new_part, old_part = jnp.exp2(shift - best), jnp.exp2(old_shift - best)
            out = acc[:, :VDIM] * new_part + old[:, :VDIM] * old_part
            total = acc[:, VDIM:] * new_part + old[:, VDIM:] * old_part
            shift = best
        else:
            out, total = acc[:, :VDIM], acc[:, VDIM:]
            shift = jnp.where(total == 0.0, MASKED, shift)
        if not last:
            o_refs[0][h, :, :VDIM] = out
            o_refs[0][h, :, VDIM:] = total
            o_refs[1][h] = shift
            return
        none = total == 0.0
        safe = jnp.where(none, 1.0, total)
        out = out / safe
        lse = jnp.where(none, MASKED, jnp.log2(safe) + shift)
        for i in range(n):
            store_piece(o_refs[i], h, out[i * PIECE : (i + 1) * PIECE], lse[i * PIECE : (i + 1) * PIECE])

    def quick(masked):
        pos = positions() if masked else None

        def one(h, fine):
            q = queries(h)
            acc = None
            for k, v, base in blocks:
                wide = slots // STEP if len(blocks) == 1 else 1
                weights = []
                for c in range(slots // STEP):
                    p = jnp.exp2(scores(q, k, h, c))
                    if masked:
                        p = jnp.where(seen(pos, base, c), p, 0.0)
                    weights.append(p.astype(BF16))
                    if len(weights) < wide:
                        continue
                    rows_of_v = v[h, (c + 1 - wide) * STEP : (c + 1) * STEP]
                    term = jnp.dot(jnp.concatenate(weights, axis=1), rows_of_v, preferred_element_type=F32)
                    acc = term if acc is None else acc + term
                    weights = []
            total = acc[:, VDIM:]
            good = (total > 1e-27) & (total < 1e30)
            if masked:
                good = good | (pos < first)
            finish(h, acc, 0.0)
            return jnp.minimum(fine, good.astype(F32).reshape(rows // 8, 8, VDIM).min(axis=0))

        return jnp.min(lax.fori_loop(0, HALF, one, jnp.ones((8, VDIM), F32)))

    def careful():
        pos = positions()

        def one(h, _):
            q = queries(h)
            best = jnp.full((rows, 1), MASKED, F32)
            for k, v, base in blocks:
                for c in range(slots // STEP):
                    s = jnp.where(seen(pos, base, c), scores(q, k, h, c), MASKED)
                    best = jnp.maximum(best, jnp.max(s, axis=1, keepdims=True))
            acc = jnp.zeros((rows, 2 * VDIM), F32)
            for k, v, base in blocks:
                for c in range(slots // STEP):
                    p = jnp.where(seen(pos, base, c), jnp.exp2(scores(q, k, h, c) - best), 0.0)
                    acc += jnp.dot(p.astype(BF16), v[h, c * STEP : (c + 1) * STEP], preferred_element_type=F32)
            finish(h, acc, best)
            return 0

        lax.fori_loop(0, HALF, one, 0)

    everything = final <= start
    nothing = first > start + 16 * TOK - 1

    @pl.when(nothing)
    def _():
        def one(h, _):
            finish(h, jnp.zeros((rows, 2 * VDIM), F32), MASKED)
            return 0

        lax.fori_loop(0, HALF, one, 0)

    @pl.when(everything)
    def _():
        good = quick(False)

        @pl.when(good < 0.5)
        def _():
            careful()

    @pl.when(jnp.logical_not(everything | nothing))
    def _():
        good = quick(True)

        @pl.when(good < 0.5)
        def _():
            careful()


def attention(spot, places, pieces, keys_vals, bases, mixed, carry=(), last=False):
    n = len(pieces)
    slots = keys_vals[0].shape[2]
    if last:
        shapes = [jax.ShapeDtypeStruct((ROWS, HALF * VDIM), BF16)] * n
    else:
        shapes = [
            jax.ShapeDtypeStruct((HALF, n * PIECE, 2 * VDIM), F32),
            jax.ShapeDtypeStruct((HALF, n * PIECE, VDIM), F32),
        ]
    return pl.pallas_call(
        functools.partial(attention_kernel, places, len(carry) > 0, last, bases, mixed),
        in_specs=[SMEM] + vmem(n + len(keys_vals) + len(carry)),
        out_specs=vmem(len(shapes)),
        out_shape=shapes,
        cost_estimate=pl.CostEstimate(
            flops=len(keys_vals) * HALF * n * PIECE * slots * 512,
            bytes_accessed=4 << 20,
            transcendentals=HALF * n * PIECE * 2 * slots,
        ),
        compiler_params=pltpu.CompilerParams(vmem_limit_bytes=VMEM),
        name="attention",
    )(spot, *pieces, *keys_vals, *carry)


def join_kernel(n, *refs):
    pieces, o_ref = refs[:n], refs[n]
    logs = [sum(p[PIECE + j : PIECE + j + 1].astype(F32) for j in range(3)) for p in pieces]
    best = functools.reduce(jnp.maximum, logs)
    shares = [jnp.exp2(v - best) for v in logs]
    total = sum(shares)
    stack = jnp.concatenate([s / total for s in shares] + [jnp.zeros((-n % 8, HALF * VDIM), F32)][: -n % 8], axis=0)
    for h in range(HALF):
        lane = slice(h * VDIM, (h + 1) * VDIM)
        cols = stack[:, lane].T
        out = sum(p[:PIECE, lane].astype(F32) * cols[:, i : i + 1] for i, p in enumerate(pieces))
        o_ref[:, lane] = out.astype(BF16)


def join(pieces):
    n = len(pieces)
    return pl.pallas_call(
        functools.partial(join_kernel, n),
        in_specs=vmem(n),
        out_specs=vmem(1)[0],
        out_shape=jax.ShapeDtypeStruct((PIECE, HALF * VDIM), BF16),
        cost_estimate=pl.CostEstimate(flops=1 << 20, bytes_accessed=1 << 20, transcendentals=4096),
        compiler_params=pltpu.CompilerParams(vmem_limit_bytes=8 << 20),
        name="join",
    )(*pieces)


def project_kernel(step, flip, spot_ref, mine_ref, theirs_ref, w_ref, o_ref):
    core, x, zhi = spot_ref[1], spot_ref[3], spot_ref[4]
    wide = o_ref.shape[1]
    rows = HALF * VDIM
    top = pl.ds(pl.multiple_of(core * rows, rows), rows)
    low = pl.ds(pl.multiple_of((1 - core) * rows, rows), rows)
    column = lanes((zhi ^ flip) * 4 + ((x + step) & 3), wide)
    acc = jnp.dot(mine_ref[:TOK], w_ref[top, column], preferred_element_type=F32)
    acc += jnp.dot(theirs_ref[...], w_ref[low, column], preferred_element_type=F32)
    o_ref[...] = acc.astype(BF16)


def project(spot, mine, theirs, w_o, step, flip):
    wide = w_o.shape[1] // 8
    return pl.pallas_call(
        functools.partial(project_kernel, step, flip),
        in_specs=[SMEM] + vmem(3),
        out_specs=vmem(1)[0],
        out_shape=jax.ShapeDtypeStruct((TOK, wide), BF16),
        cost_estimate=pl.CostEstimate(
            flops=2 * 256 * wide * 1024, bytes_accessed=2 << 20, transcendentals=0
        ),
        compiler_params=pltpu.CompilerParams(vmem_limit_bytes=12 << 20),
        name="project",
    )(spot, mine, theirs, w_o)


def on_device(q_nope, q_rope, w_uk, w_uv, w_o, latent_cache, group_start):
    ctx = lax.axis_index("ctx")
    head = lax.axis_index("head")
    chip = ctx >> 1
    place = lambda dy: (((chip >> 1) + dy) & 3) * 2 + (chip & 1)
    spot = jnp.stack(
        [group_start[0], ctx & 1, chip, head & 3, head >> 2]
        + [place(dy) for dy in range(4)]
        + [ctx ^ flip for flip in range(4)]
        + [(head + step) & 1 for step in range(2)]
    ).astype(jnp.int32)
    U, PU, DU, MU = range(5, 9)
    OWN, CORES, ZNEAR, ZCORES = range(9, 13)
    cache_other = to_ctx(latent_cache, CORE)
    keep, give, half, share = split_queries(q_nope, q_rope, latent_cache)
    z_share = to_ctx(share, ZLO)
    given = to_ctx(give, CORE)
    u = jnp.concatenate([keep, given], axis=0)
    d_u = to_ctx(u, Y2)
    p_u = to_ctx(u, YM)
    m_u = to_ctx(u, YP)
    cache_other, half = lax.optimization_barrier((cache_other, half))
    z_half = to_ctx(half, ZLO)
    near = near_keys_values(latent_cache, cache_other, w_uk, w_uv)
    z_share, near = lax.optimization_barrier((z_share, near))
    *near, uk, uv = near
    shares = [z_share, to_head(z_share, XSIDE)]

    places, pieces = (U, DU, PU, MU), (u, d_u, p_u, m_u)
    carry = attention(spot, places, pieces, near, (OWN, CORES), False)
    shares, z_half, carry = lax.optimization_barrier((shares, z_half, carry))
    z_cache = jnp.concatenate([z_half] + shares, axis=1)
    zc_cache = to_ctx(z_cache, CORE)
    carry = attention(spot, places, pieces, far_keys_values(z_cache, uk, uv), (ZNEAR,), True, carry)
    zc_cache, carry = lax.optimization_barrier((zc_cache, carry))
    r_u, r_d, r_p, r_m = attention(
        spot, places, pieces, far_keys_values(zc_cache, uk, uv), (ZCORES,), True, carry, True
    )
    mine = join([r_u, to_ctx(r_d, Y2), to_ctx(r_p, YP), to_ctx(r_m, YM)])

    theirs = to_ctx(mine[TOK:], CORE)

    def columns(mine, flip):
        across = to_head(project(spot, mine, theirs, w_o, 2, flip), X2)
        right = to_head(project(spot, mine, theirs, w_o, 1, flip), XP)
        third = project(spot, mine, theirs, w_o, 3, flip)
        left = to_head(third, XM)
        after, _ = lax.optimization_barrier((mine, third))
        own = project(spot, after, theirs, w_o, 0, flip)
        return own, (right, across, left)

    def added(own, others):
        return own.astype(F32) + sum(part.astype(F32) for part in others)

    own, others = columns(mine, 1)
    after, own = lax.optimization_barrier((mine, own))
    last = columns(after, 0)
    back = to_head(added(own, others).astype(BF16), ZHI)
    return (added(*last) + back.astype(F32)).astype(BF16)


def solution(mesh):
    placed = (
        P("ctx", "head"),
        P("ctx", "head"),
        P("head", None, None),
        P("head", None, None),
        P("head", None),
        P(None, "ctx"),
        P(),
    )
    return jax.shard_map(
        on_device, mesh=mesh, in_specs=placed, out_specs=P("ctx", "head"), check_vma=False
    )
```

```python
import functools
import math

import jax
import jax.numpy as jnp
from jax import lax
from jax.experimental import pallas as pl
from jax.experimental.pallas import tpu as pltpu
from jax.sharding import PartitionSpec as P

LATENT = 512
ROPE = 64
NOPE = 128
VDIM = 128
HALF = 4
SLOTS = 1024
TOK = 64
PIECE = 2 * TOK
ROWS = PIECE + 16
STEP = 256
PART = SLOTS // 2
SHARE = (SLOTS - PART) // 2

F32 = jnp.float32
BF16 = jnp.bfloat16
MASKED = -1e30
SCALE2 = (NOPE + ROPE) ** (-0.5) * (0.1 * math.log(32.0) + 1.0) ** 2 * math.log2(math.e)
VMEM = 20 << 20

CORE = [(i, i ^ 1) for i in range(16)]
ZLO = [(i, i ^ 2) for i in range(16)]
YP = [(i, (i + 4) % 16) for i in range(16)]
YM = [(i, (i - 4) % 16) for i in range(16)]
Y2 = [(i, (i + 8) % 16) for i in range(16)]
DIAGP = [(i, (i + 4) % 16 ^ 2) for i in range(16)]
DIAGM = [(i, (i - 4) % 16 ^ 2) for i in range(16)]
DIAG2 = [(i, (i + 8) % 16 ^ 2) for i in range(16)]
XP = [(i, (i // 4) * 4 + (i + 1) % 4) for i in range(8)]
XM = [(i, (i // 4) * 4 + (i - 1) % 4) for i in range(8)]
X2 = [(i, (i // 4) * 4 + (i + 2) % 4) for i in range(8)]
ZHI = [(i, i ^ 4) for i in range(8)]
XSIDE = [(i, i ^ 1) for i in range(8)]


def to_ctx(array, pairs):
    return lax.ppermute(array, "ctx", pairs)


def to_head(array, pairs):
    return lax.ppermute(array, "head", pairs)


def vmem(n):
    return [pl.BlockSpec(memory_space=pltpu.VMEM)] * n


SMEM = pl.BlockSpec(memory_space=pltpu.SMEM)
HBM = pl.BlockSpec(memory_space=pltpu.HBM)


def hbm(x):
    return pltpu.with_memory_space_constraint(x, pltpu.HBM)


def lanes(index, width=128):
    return pl.ds(pl.multiple_of(index * width, 128), width)


def split_kernel(nope_ref, rope_ref, cache_ref, keep_ref, give_ref, half_ref, share_ref, sems):
    core = lax.axis_index("ctx") & 1
    odd = lax.axis_index("head") & 1
    copies = []
    for ref, side in ((give_ref, 1 - core), (keep_ref, core)):
        for source, target in (
            (nope_ref.at[:, lanes(side, HALF * NOPE)], ref.at[:, : HALF * NOPE]),
            (rope_ref.at[:, lanes(side, HALF * ROPE)], ref.at[:, HALF * NOPE :]),
        ):
            copies.append(pltpu.make_async_copy(source, target, sems.at[len(copies)]))
    mine = pl.ds(pl.multiple_of(PART + odd * SHARE, SHARE), SHARE)
    for source, target in ((cache_ref.at[:, mine], share_ref), (cache_ref.at[:, :PART], half_ref)):
        copies.append(pltpu.make_async_copy(source, target, sems.at[len(copies)]))
    for copy in copies:
        copy.start()
    for copy in copies:
        copy.wait()


def split_queries(q_nope, q_rope, cache):
    shape = jax.ShapeDtypeStruct((TOK, HALF * (NOPE + ROPE)), BF16)
    return pl.pallas_call(
        split_kernel,
        in_specs=[HBM] * 3,
        out_specs=vmem(4),
        out_shape=[shape, shape] + [jax.ShapeDtypeStruct((LATENT + ROPE, n), BF16) for n in (PART, SHARE)],
        scratch_shapes=[pltpu.SemaphoreType.DMA((6,))],
        compiler_params=pltpu.CompilerParams(vmem_limit_bytes=4 << 20),
        name="split_queries",
    )(hbm(q_nope), hbm(q_rope), hbm(cache))


def form(cache, uk, uv, key_ref, val_ref):
    slots = cache.shape[1]
    latent = cache[:LATENT]
    rope = cache[LATENT:]
    blank = jnp.zeros((ROPE, slots), BF16)
    ones = jnp.ones((slots, VDIM), BF16)
    keys = jnp.dot(uk[...].reshape(HALF * NOPE, LATENT), latent, preferred_element_type=F32).astype(BF16)
    up = jnp.concatenate([uv[h] for h in range(HALF)], axis=1)
    vals = jnp.dot(latent.T, up, preferred_element_type=F32).astype(BF16)
    for h in range(HALF):
        key_ref[h, :NOPE] = keys[h * NOPE : (h + 1) * NOPE]
        key_ref[h, NOPE : NOPE + ROPE] = rope if h % 2 == 0 else blank
        key_ref[h, NOPE + ROPE :] = blank if h % 2 == 0 else rope
        val_ref[h, :, :VDIM] = vals[:, h * VDIM : (h + 1) * VDIM]
        val_ref[h, :, VDIM:] = ones


def near_kernel(cache_ref, other_ref, uk_ref, uv_ref, key0, val0, key1, val1, uk, uv, own, sems):
    heads = pl.ds((lax.axis_index("ctx") & 1) * HALF, HALF)
    copies = [
        pltpu.make_async_copy(source, target, sems.at[i])
        for i, (source, target) in enumerate(((uk_ref.at[heads], uk), (uv_ref.at[heads], uv), (cache_ref, own)))
    ]
    for copy in copies:
        copy.start()
    copies[0].wait()
    copies[1].wait()
    form(other_ref, uk, uv, key1, val1)
    copies[2].wait()
    form(own, uk, uv, key0, val0)


def kv_shapes(slots):
    return [jax.ShapeDtypeStruct((HALF, 256, slots), BF16), jax.ShapeDtypeStruct((HALF, slots, 256), BF16)]


def kv_cost(slots):
    return pl.CostEstimate(flops=4 * HALF * NOPE * LATENT * slots, bytes_accessed=4 << 20, transcendentals=0)


def near_keys_values(cache, other, w_uk, w_uv):
    uk = jax.ShapeDtypeStruct((HALF, NOPE, LATENT), BF16)
    uv = jax.ShapeDtypeStruct((HALF, LATENT, VDIM), BF16)
    return pl.pallas_call(
        near_kernel,
        in_specs=[HBM] + vmem(1) + [HBM] * 2,
        out_specs=vmem(6),
        out_shape=kv_shapes(SLOTS) * 2 + [uk, uv],
        scratch_shapes=[pltpu.VMEM((LATENT + ROPE, SLOTS), BF16), pltpu.SemaphoreType.DMA((3,))],
        cost_estimate=kv_cost(2 * SLOTS),
        compiler_params=pltpu.CompilerParams(vmem_limit_bytes=12 << 20),
        name="near_keys_values",
    )(hbm(cache), other, hbm(w_uk), hbm(w_uv))


def far_keys_values(cache, uk, uv):
    slots = cache.shape[1]
    return pl.pallas_call(
        form,
        in_specs=vmem(3),
        out_specs=vmem(2),
        out_shape=kv_shapes(slots),
        cost_estimate=kv_cost(slots),
        compiler_params=pltpu.CompilerParams(vmem_limit_bytes=12 << 20),
        name="far_keys_values",
    )(cache, uk, uv)


def split3(x):
    a = x.astype(BF16)
    r = x - a.astype(F32)
    b = r.astype(BF16)
    return a, b, (r - b.astype(F32)).astype(BF16)


def store_piece(o_ref, h, out, lse):
    o_ref[:PIECE, lanes(h)] = out.astype(BF16)
    row = lse.T[:1]
    a, b, c = split3(row)
    index = lax.broadcasted_iota(jnp.int32, (16, PIECE), 0)
    spread = lambda v: jnp.broadcast_to(v.astype(F32), (16, PIECE))
    pick = jnp.where(index == 0, spread(a), jnp.where(index == 1, spread(b), jnp.where(index == 2, spread(c), 0.0)))
    o_ref[PIECE:, lanes(h)] = pick.astype(BF16)


def attention_kernel(places, carried, last, bases, mixed, spot_ref, *refs):
    n = len(places)
    rows = n * PIECE
    m = n + 2 * len(bases)
    q_refs, kv_refs, refs = refs[:n], refs[n:m], refs[m:]
    carry, o_refs = (refs[:2], refs[2:]) if carried else (None, refs)
    start = spot_ref[0]
    core = spot_ref[1]
    slots = kv_refs[0].shape[2]
    blocks = [(kv_refs[2 * i], kv_refs[2 * i + 1], spot_ref[b] * SLOTS) for i, b in enumerate(bases)]
    first = functools.reduce(jnp.minimum, [b for _, _, b in blocks])
    final = functools.reduce(jnp.maximum, [b for _, _, b in blocks]) + slots - 1

    def queries(h):
        tall = lambda lane: jnp.concatenate([q[:, lane] for q in q_refs], axis=0)
        return jnp.concatenate([tall(lanes(h)), tall(lanes(HALF + h // 2))], axis=1)

    def positions():
        place = lax.broadcasted_iota(jnp.int32, (PIECE, 1), 0)
        mine = place < TOK
        inner = jnp.where(mine, place, place - TOK)
        side = jnp.where(mine, core, 1 - core)
        local = start + inner + side * TOK
        return jnp.concatenate([local + spot_ref[i] * PIECE for i in places], axis=0)

    def scores(q, k, h, c):
        return jnp.dot(q, k[h, :, c * STEP : (c + 1) * STEP], preferred_element_type=F32) * SCALE2

    def seen(pos, base, c):
        at = c * STEP
        if mixed and at >= PART:
            at = PART + spot_ref[13 + (at - PART) // SHARE] * SHARE
        key = base + at + lax.broadcasted_iota(jnp.int32, (1, STEP), 1)
        return key <= pos

    def finish(h, acc, shift):
        if carried:
            old, old_shift = carry[0][h], carry[1][h]
            shift = jnp.where(acc[:, VDIM:] == 0.0, MASKED, shift)
            best = jnp.maximum(shift, old_shift)
            new_part, old_part = jnp.exp2(shift - best), jnp.exp2(old_shift - best)
            out = acc[:, :VDIM] * new_part + old[:, :VDIM] * old_part
            total = acc[:, VDIM:] * new_part + old[:, VDIM:] * old_part
            shift = best
        else:
            out, total = acc[:, :VDIM], acc[:, VDIM:]
            shift = jnp.where(total == 0.0, MASKED, shift)
        if not last:
            o_refs[0][h, :, :VDIM] = out
            o_refs[0][h, :, VDIM:] = total
            o_refs[1][h] = shift
            return
        none = total == 0.0
        safe = jnp.where(none, 1.0, total)
        out = out / safe
        lse = jnp.where(none, MASKED, jnp.log2(safe) + shift)
        for i in range(n):
            store_piece(o_refs[i], h, out[i * PIECE : (i + 1) * PIECE], lse[i * PIECE : (i + 1) * PIECE])

    def quick(masked):
        pos = positions() if masked else None

        def one(h, fine):
            q = queries(h)
            acc = None
            for k, v, base in blocks:
                wide = slots // STEP if len(blocks) == 1 else 1
                weights = []
                for c in range(slots // STEP):
                    p = jnp.exp2(scores(q, k, h, c))
                    if masked:
                        p = jnp.where(seen(pos, base, c), p, 0.0)
                    weights.append(p.astype(BF16))
                    if len(weights) < wide:
                        continue
                    rows_of_v = v[h, (c + 1 - wide) * STEP : (c + 1) * STEP]
                    term = jnp.dot(jnp.concatenate(weights, axis=1), rows_of_v, preferred_element_type=F32)
                    acc = term if acc is None else acc + term
                    weights = []
            total = acc[:, VDIM:]
            good = (total > 1e-27) & (total < 1e30)
            if masked:
                good = good | (pos < first)
            finish(h, acc, 0.0)
            return jnp.minimum(fine, good.astype(F32).reshape(rows // 8, 8, VDIM).min(axis=0))

        return jnp.min(lax.fori_loop(0, HALF, one, jnp.ones((8, VDIM), F32)))

    def careful():
        pos = positions()

        def one(h, _):
            q = queries(h)
            best = jnp.full((rows, 1), MASKED, F32)
            for k, v, base in blocks:
                for c in range(slots // STEP):
                    s = jnp.where(seen(pos, base, c), scores(q, k, h, c), MASKED)
                    best = jnp.maximum(best, jnp.max(s, axis=1, keepdims=True))
            acc = jnp.zeros((rows, 2 * VDIM), F32)
            for k, v, base in blocks:
                for c in range(slots // STEP):
                    p = jnp.where(seen(pos, base, c), jnp.exp2(scores(q, k, h, c) - best), 0.0)
                    acc += jnp.dot(p.astype(BF16), v[h, c * STEP : (c + 1) * STEP], preferred_element_type=F32)
            finish(h, acc, best)
            return 0

        lax.fori_loop(0, HALF, one, 0)

    everything = final <= start
    nothing = first > start + 16 * TOK - 1

    @pl.when(nothing)
    def _():
        def one(h, _):
            finish(h, jnp.zeros((rows, 2 * VDIM), F32), MASKED)
            return 0

        lax.fori_loop(0, HALF, one, 0)

    @pl.when(everything)
    def _():
        good = quick(False)

        @pl.when(good < 0.5)
        def _():
            careful()

    @pl.when(jnp.logical_not(everything | nothing))
    def _():
        good = quick(True)

        @pl.when(good < 0.5)
        def _():
            careful()


def attention(spot, places, pieces, keys_vals, bases, mixed, carry=(), last=False):
    n = len(pieces)
    slots = keys_vals[0].shape[2]
    if last:
        shapes = [jax.ShapeDtypeStruct((ROWS, HALF * VDIM), BF16)] * n
    else:
        shapes = [
            jax.ShapeDtypeStruct((HALF, n * PIECE, 2 * VDIM), F32),
            jax.ShapeDtypeStruct((HALF, n * PIECE, VDIM), F32),
        ]
    return pl.pallas_call(
        functools.partial(attention_kernel, places, len(carry) > 0, last, bases, mixed),
        in_specs=[SMEM] + vmem(n + len(keys_vals) + len(carry)),
        out_specs=vmem(len(shapes)),
        out_shape=shapes,
        cost_estimate=pl.CostEstimate(
            flops=len(keys_vals) * HALF * n * PIECE * slots * 512,
            bytes_accessed=4 << 20,
            transcendentals=HALF * n * PIECE * 2 * slots,
        ),
        compiler_params=pltpu.CompilerParams(vmem_limit_bytes=VMEM),
        name="attention",
    )(spot, *pieces, *keys_vals, *carry)


def join_kernel(n, *refs):
    pieces, o_ref = refs[:n], refs[n]
    logs = [sum(p[PIECE + j : PIECE + j + 1].astype(F32) for j in range(3)) for p in pieces]
    best = functools.reduce(jnp.maximum, logs)
    shares = [jnp.exp2(v - best) for v in logs]
    total = sum(shares)
    stack = jnp.concatenate([s / total for s in shares] + [jnp.zeros((-n % 8, HALF * VDIM), F32)][: -n % 8], axis=0)
    for h in range(HALF):
        lane = slice(h * VDIM, (h + 1) * VDIM)
        cols = stack[:, lane].T
        out = sum(p[:PIECE, lane].astype(F32) * cols[:, i : i + 1] for i, p in enumerate(pieces))
        o_ref[:, lane] = out.astype(BF16)


def join(pieces):
    n = len(pieces)
    return pl.pallas_call(
        functools.partial(join_kernel, n),
        in_specs=vmem(n),
        out_specs=vmem(1)[0],
        out_shape=jax.ShapeDtypeStruct((PIECE, HALF * VDIM), BF16),
        cost_estimate=pl.CostEstimate(flops=1 << 20, bytes_accessed=1 << 20, transcendentals=4096),
        compiler_params=pltpu.CompilerParams(vmem_limit_bytes=8 << 20),
        name="join",
    )(*pieces)


def project_kernel(blocks, spot_ref, mine_ref, theirs_ref, w_ref, *o_refs):
    core, x, zhi = spot_ref[1], spot_ref[3], spot_ref[4]
    rows = HALF * VDIM
    top = pl.ds(pl.multiple_of(core * rows, rows), rows)
    low = pl.ds(pl.multiple_of((1 - core) * rows, rows), rows)
    for (step, flip), o_ref in zip(blocks, o_refs):
        column = lanes((zhi ^ flip) * 4 + ((x + step) & 3), o_ref.shape[1])
        acc = jnp.dot(mine_ref[:TOK], w_ref[top, column], preferred_element_type=F32)
        acc += jnp.dot(theirs_ref[...], w_ref[low, column], preferred_element_type=F32)
        o_ref[...] = acc.astype(BF16)


def project(spot, mine, theirs, w_o, blocks):
    n, wide = len(blocks), w_o.shape[1] // 8
    return pl.pallas_call(
        functools.partial(project_kernel, blocks),
        in_specs=[SMEM] + vmem(3),
        out_specs=vmem(n),
        out_shape=[jax.ShapeDtypeStruct((TOK, wide), BF16)] * n,
        cost_estimate=pl.CostEstimate(
            flops=2 * n * 256 * wide * 1024, bytes_accessed=n << 21, transcendentals=0
        ),
        compiler_params=pltpu.CompilerParams(vmem_limit_bytes=12 << 20),
        name="project",
    )(spot, mine, theirs, w_o)


def on_device(q_nope, q_rope, w_uk, w_uv, w_o, latent_cache, group_start):
    ctx = lax.axis_index("ctx")
    head = lax.axis_index("head")
    chip = ctx >> 1
    place = lambda dy: (((chip >> 1) + dy) & 3) * 2 + (chip & 1)
    spot = jnp.stack(
        [group_start[0], ctx & 1, chip, head & 3, head >> 2]
        + [place(dy) for dy in range(4)]
        + [ctx ^ flip for flip in range(4)]
        + [(head + step) & 1 for step in range(2)]
    ).astype(jnp.int32)
    U, PU, DU, MU = range(5, 9)
    OWN, CORES, ZNEAR, ZCORES = range(9, 13)
    cache_other = to_ctx(latent_cache, CORE)
    keep, give, half, share = split_queries(q_nope, q_rope, latent_cache)
    z_share = to_ctx(share, ZLO)
    given = to_ctx(give, CORE)
    u = jnp.concatenate([keep, given], axis=0)
    d_u = to_ctx(u, Y2)
    p_u = to_ctx(u, YM)
    m_u = to_ctx(u, YP)
    cache_other, half = lax.optimization_barrier((cache_other, half))
    z_half = to_ctx(half, ZLO)
    near = near_keys_values(latent_cache, cache_other, w_uk, w_uv)
    z_share, near = lax.optimization_barrier((z_share, near))
    *near, uk, uv = near
    shares = [z_share, to_head(z_share, XSIDE)]

    places, pieces = (U, DU, PU, MU), (u, d_u, p_u, m_u)
    carry = attention(spot, places, pieces, near, (OWN, CORES), False)
    shares, z_half, carry = lax.optimization_barrier((shares, z_half, carry))
    z_cache = jnp.concatenate([z_half] + shares, axis=1)
    zc_cache = to_ctx(z_cache, CORE)
    carry = attention(spot, places, pieces, far_keys_values(z_cache, uk, uv), (ZNEAR,), True, carry)
    zc_cache, carry = lax.optimization_barrier((zc_cache, carry))
    r_u, r_d, r_p, r_m = attention(
        spot, places, pieces, far_keys_values(zc_cache, uk, uv), (ZCORES,), True, carry, True
    )
    mine = join([r_u, to_ctx(r_d, Y2), to_ctx(r_p, YP), to_ctx(r_m, YM)])

    theirs = to_ctx(mine[TOK:], CORE)

    def after(*earlier):
        return lax.optimization_barrier((mine, *earlier))[0]

    (far2,) = project(spot, mine, theirs, w_o, ((2, 1),))
    far1, far3 = project(spot, after(far2), theirs, w_o, ((1, 1), (3, 1)))
    own1, own3 = project(spot, after(far1), theirs, w_o, ((1, 0), (3, 0)))
    own2, far0, own0 = project(spot, after(own1), theirs, w_o, ((2, 0), (0, 1), (0, 0)))

    def summed(own, right, across, left):
        parts = (to_head(across, X2), to_head(right, XP), to_head(left, XM))
        return own.astype(F32) + sum(part.astype(F32) for part in parts)

    back = to_head(summed(far0, far1, far2, far3).astype(BF16), ZHI)
    return (summed(own0, own1, own2, own3) + back.astype(F32)).astype(BF16)


def solution(mesh):
    placed = (
        P("ctx", "head"),
        P("ctx", "head"),
        P("head", None, None),
        P("head", None, None),
        P("head", None),
        P(None, "ctx"),
        P(),
    )
    return jax.shard_map(
        on_device, mesh=mesh, in_specs=placed, out_specs=P("ctx", "head"), check_vma=False
    )
```

```python
import functools
import math

import jax
import jax.numpy as jnp
from jax import lax
from jax.experimental import pallas as pl
from jax.experimental.pallas import tpu as pltpu
from jax.sharding import PartitionSpec as P

LATENT = 512
ROPE = 64
NOPE = 128
VDIM = 128
HALF = 4
SLOTS = 1024
TOK = 64
PIECE = 2 * TOK
ROWS = PIECE + 16
STEP = 256
PART = SLOTS // 2
SHARE = (SLOTS - PART) // 2

F32 = jnp.float32
BF16 = jnp.bfloat16
MASKED = -1e30
SCALE2 = (NOPE + ROPE) ** (-0.5) * (0.1 * math.log(32.0) + 1.0) ** 2 * math.log2(math.e)
VMEM = 20 << 20

CORE = [(i, i ^ 1) for i in range(16)]
ZLO = [(i, i ^ 2) for i in range(16)]
YP = [(i, (i + 4) % 16) for i in range(16)]
YM = [(i, (i - 4) % 16) for i in range(16)]
Y2 = [(i, (i + 8) % 16) for i in range(16)]
DIAGP = [(i, (i + 4) % 16 ^ 2) for i in range(16)]
DIAGM = [(i, (i - 4) % 16 ^ 2) for i in range(16)]
DIAG2 = [(i, (i + 8) % 16 ^ 2) for i in range(16)]
XP = [(i, (i // 4) * 4 + (i + 1) % 4) for i in range(8)]
XM = [(i, (i // 4) * 4 + (i - 1) % 4) for i in range(8)]
X2 = [(i, (i // 4) * 4 + (i + 2) % 4) for i in range(8)]
ZHI = [(i, i ^ 4) for i in range(8)]
XSIDE = [(i, i ^ 1) for i in range(8)]


def to_ctx(array, pairs):
    return lax.ppermute(array, "ctx", pairs)


def to_head(array, pairs):
    return lax.ppermute(array, "head", pairs)


def vmem(n):
    return [pl.BlockSpec(memory_space=pltpu.VMEM)] * n


SMEM = pl.BlockSpec(memory_space=pltpu.SMEM)
HBM = pl.BlockSpec(memory_space=pltpu.HBM)


def hbm(x):
    return pltpu.with_memory_space_constraint(x, pltpu.HBM)


def lanes(index, width=128):
    return pl.ds(pl.multiple_of(index * width, 128), width)


def split_kernel(nope_ref, rope_ref, cache_ref, keep_ref, give_ref, half_ref, share_ref, sems):
    core = lax.axis_index("ctx") & 1
    odd = lax.axis_index("head") & 1
    copies = []
    for ref, side in ((give_ref, 1 - core), (keep_ref, core)):
        for source, target in (
            (nope_ref.at[:, lanes(side, HALF * NOPE)], ref.at[:, : HALF * NOPE]),
            (rope_ref.at[:, lanes(side, HALF * ROPE)], ref.at[:, HALF * NOPE :]),
        ):
            copies.append(pltpu.make_async_copy(source, target, sems.at[len(copies)]))
    mine = pl.ds(pl.multiple_of(PART + odd * SHARE, SHARE), SHARE)
    for source, target in ((cache_ref.at[:, mine], share_ref), (cache_ref.at[:, :PART], half_ref)):
        copies.append(pltpu.make_async_copy(source, target, sems.at[len(copies)]))
    for copy in copies:
        copy.start()
    for copy in copies:
        copy.wait()


def split_queries(q_nope, q_rope, cache):
    shape = jax.ShapeDtypeStruct((TOK, HALF * (NOPE + ROPE)), BF16)
    return pl.pallas_call(
        split_kernel,
        in_specs=[HBM] * 3,
        out_specs=vmem(4),
        out_shape=[shape, shape] + [jax.ShapeDtypeStruct((LATENT + ROPE, n), BF16) for n in (PART, SHARE)],
        scratch_shapes=[pltpu.SemaphoreType.DMA((6,))],
        compiler_params=pltpu.CompilerParams(vmem_limit_bytes=4 << 20),
        name="split_queries",
    )(hbm(q_nope), hbm(q_rope), hbm(cache))


def form(cache, uk, uv, key_ref, val_ref):
    slots = cache.shape[1]
    latent = cache[:LATENT]
    rope = cache[LATENT:]
    blank = jnp.zeros((ROPE, slots), BF16)
    ones = jnp.ones((slots, VDIM), BF16)
    keys = jnp.dot(uk[...].reshape(HALF * NOPE, LATENT), latent, preferred_element_type=F32).astype(BF16)
    up = jnp.concatenate([uv[h] for h in range(HALF)], axis=1)
    vals = jnp.dot(latent.T, up, preferred_element_type=F32).astype(BF16)
    for h in range(HALF):
        key_ref[h, :NOPE] = keys[h * NOPE : (h + 1) * NOPE]
        key_ref[h, NOPE : NOPE + ROPE] = rope if h % 2 == 0 else blank
        key_ref[h, NOPE + ROPE :] = blank if h % 2 == 0 else rope
        val_ref[h, :, :VDIM] = vals[:, h * VDIM : (h + 1) * VDIM]
        val_ref[h, :, VDIM:] = ones


def near_kernel(cache_ref, other_ref, uk_ref, uv_ref, key0, val0, key1, val1, uk, uv, own, sems):
    heads = pl.ds((lax.axis_index("ctx") & 1) * HALF, HALF)
    copies = [
        pltpu.make_async_copy(source, target, sems.at[i])
        for i, (source, target) in enumerate(((uk_ref.at[heads], uk), (uv_ref.at[heads], uv), (cache_ref, own)))
    ]
    for copy in copies:
        copy.start()
    copies[0].wait()
    copies[1].wait()
    form(other_ref, uk, uv, key1, val1)
    copies[2].wait()
    form(own, uk, uv, key0, val0)


def kv_shapes(slots):
    return [jax.ShapeDtypeStruct((HALF, 256, slots), BF16), jax.ShapeDtypeStruct((HALF, slots, 256), BF16)]


def kv_cost(slots):
    return pl.CostEstimate(flops=4 * HALF * NOPE * LATENT * slots, bytes_accessed=4 << 20, transcendentals=0)


def near_keys_values(cache, other, w_uk, w_uv):
    uk = jax.ShapeDtypeStruct((HALF, NOPE, LATENT), BF16)
    uv = jax.ShapeDtypeStruct((HALF, LATENT, VDIM), BF16)
    return pl.pallas_call(
        near_kernel,
        in_specs=[HBM] + vmem(1) + [HBM] * 2,
        out_specs=vmem(6),
        out_shape=kv_shapes(SLOTS) * 2 + [uk, uv],
        scratch_shapes=[pltpu.VMEM((LATENT + ROPE, SLOTS), BF16), pltpu.SemaphoreType.DMA((3,))],
        cost_estimate=kv_cost(2 * SLOTS),
        compiler_params=pltpu.CompilerParams(vmem_limit_bytes=12 << 20),
        name="near_keys_values",
    )(hbm(cache), other, hbm(w_uk), hbm(w_uv))


def far_keys_values(cache, uk, uv):
    slots = cache.shape[1]
    return pl.pallas_call(
        form,
        in_specs=vmem(3),
        out_specs=vmem(2),
        out_shape=kv_shapes(slots),
        cost_estimate=kv_cost(slots),
        compiler_params=pltpu.CompilerParams(vmem_limit_bytes=12 << 20),
        name="far_keys_values",
    )(cache, uk, uv)


def split3(x):
    a = x.astype(BF16)
    r = x - a.astype(F32)
    b = r.astype(BF16)
    return a, b, (r - b.astype(F32)).astype(BF16)


def store_piece(o_ref, h, out, lse):
    o_ref[:PIECE, lanes(h)] = out.astype(BF16)
    row = lse.T[:1]
    a, b, c = split3(row)
    index = lax.broadcasted_iota(jnp.int32, (16, PIECE), 0)
    spread = lambda v: jnp.broadcast_to(v.astype(F32), (16, PIECE))
    pick = jnp.where(index == 0, spread(a), jnp.where(index == 1, spread(b), jnp.where(index == 2, spread(c), 0.0)))
    o_ref[PIECE:, lanes(h)] = pick.astype(BF16)


def attention_kernel(places, carried, last, bases, mixed, spot_ref, *refs):
    n = len(places)
    rows = n * PIECE
    m = n + 2 * len(bases)
    q_refs, kv_refs, refs = refs[:n], refs[n:m], refs[m:]
    carry, o_refs = (refs[:2], refs[2:]) if carried else (None, refs)
    start = spot_ref[0]
    core = spot_ref[1]
    slots = kv_refs[0].shape[2]
    blocks = [(kv_refs[2 * i], kv_refs[2 * i + 1], spot_ref[b] * SLOTS) for i, b in enumerate(bases)]
    first = functools.reduce(jnp.minimum, [b for _, _, b in blocks])
    final = functools.reduce(jnp.maximum, [b for _, _, b in blocks]) + slots - 1

    def queries(h):
        tall = lambda lane: jnp.concatenate([q[:, lane] for q in q_refs], axis=0)
        return jnp.concatenate([tall(lanes(h)), tall(lanes(HALF + h // 2))], axis=1)

    def positions():
        place = lax.broadcasted_iota(jnp.int32, (PIECE, 1), 0)
        mine = place < TOK
        inner = jnp.where(mine, place, place - TOK)
        side = jnp.where(mine, core, 1 - core)
        local = start + inner + side * TOK
        return jnp.concatenate([local + spot_ref[i] * PIECE for i in places], axis=0)

    def scores(q, k, h, c):
        return jnp.dot(q, k[h, :, c * STEP : (c + 1) * STEP], preferred_element_type=F32) * SCALE2

    def seen(pos, base, c):
        at = c * STEP
        if mixed and at >= PART:
            at = PART + spot_ref[13 + (at - PART) // SHARE] * SHARE
        key = base + at + lax.broadcasted_iota(jnp.int32, (1, STEP), 1)
        return key <= pos

    def finish(h, acc, shift):
        if carried:
            old, old_shift = carry[0][h], carry[1][h]
            shift = jnp.where(acc[:, VDIM:] == 0.0, MASKED, shift)
            best = jnp.maximum(shift, old_shift)
            new_part, old_part = jnp.exp2(shift - best), jnp.exp2(old_shift - best)
            out = acc[:, :VDIM] * new_part + old[:, :VDIM] * old_part
            total = acc[:, VDIM:] * new_part + old[:, VDIM:] * old_part
            shift = best
        else:
            out, total = acc[:, :VDIM], acc[:, VDIM:]
            shift = jnp.where(total == 0.0, MASKED, shift)
        if not last:
            o_refs[0][h, :, :VDIM] = out
            o_refs[0][h, :, VDIM:] = total
            o_refs[1][h] = shift
            return
        none = total == 0.0
        safe = jnp.where(none, 1.0, total)
        out = out / safe
        lse = jnp.where(none, MASKED, jnp.log2(safe) + shift)
        for i in range(n):
            store_piece(o_refs[i], h, out[i * PIECE : (i + 1) * PIECE], lse[i * PIECE : (i + 1) * PIECE])

    def quick(masked):
        pos = positions() if masked else None

        def one(h, fine):
            q = queries(h)
            acc = None
            for k, v, base in blocks:
                wide = slots // STEP if len(blocks) == 1 else 1
                weights = []
                for c in range(slots // STEP):
                    p = jnp.exp2(scores(q, k, h, c))
                    if masked:
                        p = jnp.where(seen(pos, base, c), p, 0.0)
                    weights.append(p.astype(BF16))
                    if len(weights) < wide:
                        continue
                    rows_of_v = v[h, (c + 1 - wide) * STEP : (c + 1) * STEP]
                    term = jnp.dot(jnp.concatenate(weights, axis=1), rows_of_v, preferred_element_type=F32)
                    acc = term if acc is None else acc + term
                    weights = []
            total = acc[:, VDIM:]
            good = (total > 1e-27) & (total < 1e30)
            if masked:
                good = good | (pos < first)
            finish(h, acc, 0.0)
            return jnp.minimum(fine, good.astype(F32).reshape(rows // 8, 8, VDIM).min(axis=0))

        return jnp.min(lax.fori_loop(0, HALF, one, jnp.ones((8, VDIM), F32)))

    def careful():
        pos = positions()

        def one(h, _):
            q = queries(h)
            best = jnp.full((rows, 1), MASKED, F32)
            for k, v, base in blocks:
                for c in range(slots // STEP):
                    s = jnp.where(seen(pos, base, c), scores(q, k, h, c), MASKED)
                    best = jnp.maximum(best, jnp.max(s, axis=1, keepdims=True))
            acc = jnp.zeros((rows, 2 * VDIM), F32)
            for k, v, base in blocks:
                for c in range(slots // STEP):
                    p = jnp.where(seen(pos, base, c), jnp.exp2(scores(q, k, h, c) - best), 0.0)
                    acc += jnp.dot(p.astype(BF16), v[h, c * STEP : (c + 1) * STEP], preferred_element_type=F32)
            finish(h, acc, best)
            return 0

        lax.fori_loop(0, HALF, one, 0)

    everything = final <= start
    nothing = first > start + 16 * TOK - 1

    @pl.when(nothing)
    def _():
        def one(h, _):
            finish(h, jnp.zeros((rows, 2 * VDIM), F32), MASKED)
            return 0

        lax.fori_loop(0, HALF, one, 0)

    @pl.when(everything)
    def _():
        good = quick(False)

        @pl.when(good < 0.5)
        def _():
            careful()

    @pl.when(jnp.logical_not(everything | nothing))
    def _():
        good = quick(True)

        @pl.when(good < 0.5)
        def _():
            careful()


def attention(spot, places, pieces, keys_vals, bases, mixed, carry=(), last=False):
    n = len(pieces)
    slots = keys_vals[0].shape[2]
    if last:
        shapes = [jax.ShapeDtypeStruct((ROWS, HALF * VDIM), BF16)] * n
    else:
        shapes = [
            jax.ShapeDtypeStruct((HALF, n * PIECE, 2 * VDIM), F32),
            jax.ShapeDtypeStruct((HALF, n * PIECE, VDIM), F32),
        ]
    return pl.pallas_call(
        functools.partial(attention_kernel, places, len(carry) > 0, last, bases, mixed),
        in_specs=[SMEM] + vmem(n + len(keys_vals) + len(carry)),
        out_specs=vmem(len(shapes)),
        out_shape=shapes,
        cost_estimate=pl.CostEstimate(
            flops=len(keys_vals) * HALF * n * PIECE * slots * 512,
            bytes_accessed=4 << 20,
            transcendentals=HALF * n * PIECE * 2 * slots,
        ),
        compiler_params=pltpu.CompilerParams(vmem_limit_bytes=VMEM),
        name="attention",
    )(spot, *pieces, *keys_vals, *carry)


def join_kernel(n, *refs):
    pieces, o_ref = refs[:n], refs[n]
    tails = [p[PIECE:].astype(F32) for p in pieces]
    logs = [tail[0:1] + tail[1:2] + tail[2:3] for tail in tails]
    best = functools.reduce(jnp.maximum, logs)
    shares = [jnp.exp2(v - best) for v in logs]
    total = sum(shares)
    stack = jnp.concatenate([s / total for s in shares] + [jnp.zeros((-n % 8, HALF * VDIM), F32)][: -n % 8], axis=0)
    for h in range(HALF):
        lane = slice(h * VDIM, (h + 1) * VDIM)
        cols = stack[:, lane].T
        out = sum(p[:PIECE, lane].astype(F32) * cols[:, i : i + 1] for i, p in enumerate(pieces))
        o_ref[:, lane] = out.astype(BF16)


def join(pieces):
    n = len(pieces)
    return pl.pallas_call(
        functools.partial(join_kernel, n),
        in_specs=vmem(n),
        out_specs=vmem(1)[0],
        out_shape=jax.ShapeDtypeStruct((PIECE, HALF * VDIM), BF16),
        cost_estimate=pl.CostEstimate(flops=1 << 20, bytes_accessed=1 << 20, transcendentals=4096),
        compiler_params=pltpu.CompilerParams(vmem_limit_bytes=8 << 20),
        name="join",
    )(*pieces)


def project_kernel(blocks, spot_ref, mine_ref, theirs_ref, w_ref, *o_refs):
    core, x, zhi = spot_ref[1], spot_ref[3], spot_ref[4]
    rows = HALF * VDIM
    top = pl.ds(pl.multiple_of(core * rows, rows), rows)
    low = pl.ds(pl.multiple_of((1 - core) * rows, rows), rows)
    for (step, flip), o_ref in zip(blocks, o_refs):
        column = lanes((zhi ^ flip) * 4 + ((x + step) & 3), o_ref.shape[1])
        acc = jnp.dot(mine_ref[:TOK], w_ref[top, column], preferred_element_type=F32)
        acc += jnp.dot(theirs_ref[...], w_ref[low, column], preferred_element_type=F32)
        o_ref[...] = acc.astype(BF16)


def project(spot, mine, theirs, w_o, blocks):
    n, wide = len(blocks), w_o.shape[1] // 8
    return pl.pallas_call(
        functools.partial(project_kernel, blocks),
        in_specs=[SMEM] + vmem(3),
        out_specs=vmem(n),
        out_shape=[jax.ShapeDtypeStruct((TOK, wide), BF16)] * n,
        cost_estimate=pl.CostEstimate(
            flops=2 * n * 256 * wide * 1024, bytes_accessed=n << 21, transcendentals=0
        ),
        compiler_params=pltpu.CompilerParams(vmem_limit_bytes=12 << 20),
        name="project",
    )(spot, mine, theirs, w_o)


def on_device(q_nope, q_rope, w_uk, w_uv, w_o, latent_cache, group_start):
    ctx = lax.axis_index("ctx")
    head = lax.axis_index("head")
    chip = ctx >> 1
    place = lambda dy: (((chip >> 1) + dy) & 3) * 2 + (chip & 1)
    spot = jnp.stack(
        [group_start[0], ctx & 1, chip, head & 3, head >> 2]
        + [place(dy) for dy in range(4)]
        + [ctx ^ flip for flip in range(4)]
        + [(head + step) & 1 for step in range(2)]
    ).astype(jnp.int32)
    U, PU, DU, MU = range(5, 9)
    OWN, CORES, ZNEAR, ZCORES = range(9, 13)
    cache_other = to_ctx(latent_cache, CORE)
    keep, give, half, share = split_queries(q_nope, q_rope, latent_cache)
    z_share = to_ctx(share, ZLO)
    given = to_ctx(give, CORE)
    u = jnp.concatenate([keep, given], axis=0)
    d_u = to_ctx(u, Y2)
    p_u = to_ctx(u, YM)
    m_u = to_ctx(u, YP)
    cache_other, half = lax.optimization_barrier((cache_other, half))
    z_half = to_ctx(half, ZLO)
    near = near_keys_values(latent_cache, cache_other, w_uk, w_uv)
    z_share, near = lax.optimization_barrier((z_share, near))
    *near, uk, uv = near
    shares = [z_share, to_head(z_share, XSIDE)]

    places, pieces = (U, DU, PU, MU), (u, d_u, p_u, m_u)
    carry = attention(spot, places, pieces, near, (OWN, CORES), False)
    shares, z_half, carry = lax.optimization_barrier((shares, z_half, carry))
    z_cache = jnp.concatenate([z_half] + shares, axis=1)
    zc_cache = to_ctx(z_cache, CORE)
    carry = attention(spot, places, pieces, far_keys_values(z_cache, uk, uv), (ZNEAR,), True, carry)
    zc_cache, carry = lax.optimization_barrier((zc_cache, carry))
    r_u, r_d, r_p, r_m = attention(
        spot, places, pieces, far_keys_values(zc_cache, uk, uv), (ZCORES,), True, carry, True
    )
    mine = join([r_u, to_ctx(r_d, Y2), to_ctx(r_p, YP), to_ctx(r_m, YM)])

    theirs = to_ctx(mine[TOK:], CORE)

    def after(*earlier):
        return lax.optimization_barrier((mine, *earlier))[0]

    (far2,) = project(spot, mine, theirs, w_o, ((2, 1),))
    far1, far3 = project(spot, after(far2), theirs, w_o, ((1, 1), (3, 1)))
    own1, own3 = project(spot, after(far1), theirs, w_o, ((1, 0), (3, 0)))
    own2, far0, own0 = project(spot, after(own1), theirs, w_o, ((2, 0), (0, 1), (0, 0)))

    def summed(own, right, across, left):
        parts = (to_head(across, X2), to_head(right, XP), to_head(left, XM))
        return own.astype(F32) + sum(part.astype(F32) for part in parts)

    back = to_head(summed(far0, far1, far2, far3).astype(BF16), ZHI)
    return (summed(own0, own1, own2, own3) + back.astype(F32)).astype(BF16)


def solution(mesh):
    placed = (
        P("ctx", "head"),
        P("ctx", "head"),
        P("head", None, None),
        P("head", None, None),
        P("head", None),
        P(None, "ctx"),
        P(),
    )
    return jax.shard_map(
        on_device, mesh=mesh, in_specs=placed, out_specs=P("ctx", "head"), check_vma=False
    )
```
